32 devices in a mesh: section: 4 (over y, x), col: 8 (over z, core).
Axes of the slice: x: 2, y: 2, z: 4, core: 2. Of those that a mesh axis runs over, the one named last changes fastest.
Arguments:
- features: bfloat16 [4, 32, 65536], P(None, 'section', 'col'), may hold values from -48 to 48
- weights: bfloat16 [4, 512, 4, 128, 128], P('section', 'col'), may hold values from -0.375 to 0.375
- sources: int32 [4, 512, 4], P('section', 'col'), may hold values from 0 to 511, as said below
- bias: float32 [4, 65536], P('section', 'col'), may hold values from -0.3 to 0.3
- batch_rows: int32 [4], replicated, may hold values from 1 to 32, as said below
Outputs:
- final_act: bfloat16 [4, 32, 65536], P(None, 'section', 'col')
The draws below stay inside these ranges and needn't reach their ends.
Inputs may be any that keep to these rules, and one draw needn't show every extreme that they name: In every layer, the sources of all block columns c with c // 64 = d name exactly 2 distinct blocks b with b // 64 = e, for every pair d, e. `batch_rows`: some micro-batch has exactly 32 live rows.
All inputs are finite; a program needn't handle non-finite values.
Results may differ from the reference program's by a relative error of at most 0.033.
Values may be sent and summed in bfloat16 or wider, within the bound.
No kernel may reach another device: no remote copies, remote signals or barrier semaphores. Data moves between devices by JAX's collectives and lax.ppermute only.
A program may use at most 64 MiB of HBM per device.

```python
import jax
import jax.numpy as jnp
from jax import lax

NEUR = 65536
BLK = 128
KNZ = 4
CAP = 2
ROWS = 32
M_BATCH = 4
NBLK = 512
DEV_BLK = 64
LAYERS = 4
N_COL = 8


def draw_sources(key, part):
    dev_blocks = NBLK // N_COL
    pool_size = N_COL * CAP

    def one_device(dev_key):
        keys = jax.random.split(dev_key, N_COL + 1)
        picks = jax.vmap(lambda one_key: jax.random.permutation(one_key, dev_blocks)[:CAP])(keys[:N_COL])
        offsets = dev_blocks * jnp.arange(N_COL, dtype=jnp.int32)[:, None]
        pool = (picks.astype(jnp.int32) + offsets).reshape(pool_size)
        order = jax.random.permutation(keys[N_COL], dev_blocks * KNZ).astype(jnp.int32)
        return pool[order % pool_size].reshape(dev_blocks, KNZ)

    def one_layer(layer_key):
        return jax.vmap(one_device)(jax.random.split(layer_key, N_COL)).reshape(NBLK, KNZ)
    return jax.vmap(one_layer)(jax.random.split(key, LAYERS)).astype(jnp.int32)


def draw_batch_rows(key, part):
    first_key = jax.random.fold_in(key, 11)
    second_key = jax.random.fold_in(key, 23)
    counts = jax.random.randint(first_key, (M_BATCH,), 1, ROWS + 1, dtype=jnp.int32)
    fullest = jax.random.randint(second_key, (), 0, M_BATCH, dtype=jnp.int32)
    slots = jnp.arange(M_BATCH, dtype=jnp.int32)
    return jnp.where(slots == fullest, jnp.int32(ROWS), counts).astype(jnp.int32)


def block_scale(own_key, dims, cuts, low, high):
    def one(position, blocks):
        heights = jax.random.uniform(jax.random.fold_in(jax.random.fold_in(own_key, 6), position), (blocks,), jnp.float32, low / len(cuts), high / len(cuts))
        return jnp.repeat(jnp.exp(heights), dims[position] // blocks).reshape((-1,) + (1,) * (len(dims) - position - 1))

    level = one(*cuts[0])
    for cut in cuts[1:]:
        level = level * one(*cut)
    return level


def centred(rng, dims, deviation, limit, shards=(), kind=jnp.bfloat16):
    values = deviation * jax.random.normal(rng, dims, jnp.float32)
    if shards:
        values = values * block_scale(rng, dims, shards, -0.22, 0.18)
    return jnp.clip(values, -limit, limit).astype(kind)


def setup_inputs(seed: int = 0) -> dict:
    key_list = jax.random.split(jax.random.key(seed), 6)
    features = centred(key_list[0], (M_BATCH, ROWS, NEUR), 8.0, 48.0, ((1, 4), (2, 8)))
    weights = centred(key_list[1], (LAYERS, NBLK, KNZ, BLK, BLK), (KNZ * BLK // 2) ** -0.5, 0.375, ((0, 4), (1, 8)))
    sources = draw_sources(jax.random.fold_in(key_list[5], 71), 0)
    bias = jnp.clip(jax.random.uniform(key_list[3], (LAYERS, NEUR), jnp.float32, -0.3, 0.3) * block_scale(key_list[3], (LAYERS, NEUR), ((0, 4), (1, 8)), -0.4, 0.0), -0.3, 0.3)
    batch_rows = draw_batch_rows(jax.random.fold_in(key_list[5], 71), 0)
    return dict(features=features, weights=weights, sources=sources, bias=bias, batch_rows=batch_rows)


def reference(features, weights, sources, bias, batch_rows):
    row_total = M_BATCH * ROWS
    groups = NBLK // DEV_BLK
    activity = features.reshape(row_total, NBLK, BLK).transpose(1, 0, 2)
    for layer_idx in range(LAYERS):
        layer_w = weights[layer_idx].reshape(groups, DEV_BLK, KNZ, BLK, BLK)
        layer_s = sources[layer_idx].reshape(groups, DEV_BLK, KNZ)
        layer_b = bias[layer_idx].reshape(groups, DEV_BLK, 1, BLK)

        def group_step(group_args, current=activity):
            block_w, block_s, block_b = group_args
            picked = current[block_s].astype(jnp.float32)
            preact = jnp.einsum("ckrb,ckbo->cro", picked, block_w.astype(jnp.float32))
            return jnp.clip(preact + block_b, 0.0, 32.0).astype(jnp.bfloat16)

        activity = lax.map(group_step, (layer_w, layer_s, layer_b)).reshape(NBLK, row_total, BLK)
    result = activity.transpose(1, 0, 2).reshape(M_BATCH, ROWS, NEUR)
    row_mask = jnp.arange(ROWS, dtype=jnp.int32)[None, :] < batch_rows[:, None]
    return jnp.where(row_mask[:, :, None], result, jnp.zeros_like(result)).astype(jnp.bfloat16)
```

```python
import functools

import jax
import jax.numpy as jnp
from jax import lax
from jax.experimental import pallas as pl
from jax.experimental.pallas import tpu as pltpu
from jax.sharding import PartitionSpec as P

CAP = 2
CORES = 2
BOTH = ("section", "col")
VM = pl.BlockSpec(memory_space=pltpu.VMEM)
SM = pl.BlockSpec(memory_space=pltpu.SMEM)
HB = pl.BlockSpec(memory_space=pl.ANY)
BIG = 1 << 30


def pool_kernel(cols, blocks_own, src_ref, ask_ref, slot_ref):
    src = src_ref[...]
    owner = src // blocks_own
    slot = jnp.zeros_like(src)
    lows, highs = [], []
    for e in range(cols):
        mine = owner == e
        low = jnp.min(jnp.where(mine, src, BIG), axis=(0, 1), keepdims=True)
        high = jnp.max(jnp.where(mine, src, -1), axis=(0, 1), keepdims=True)
        slot = jnp.where(mine, CAP * e + (src > low).astype(jnp.int32), slot)
        lows.append(low - e * blocks_own)
        highs.append(high - e * blocks_own)
    slot_ref[...] = slot
    ask = jnp.concatenate([jnp.concatenate([a, b], axis=1) for a, b in zip(lows, highs)], axis=0)
    for s in range(ask_ref.shape[0] // cols):
        ask_ref[s * cols : (s + 1) * cols, :] = ask


def need_kernel(sections, cols, knz, got_ref, slot_ref, info_ref):
    nxt = jnp.minimum(lax.axis_index("section") + 1, sections - 1)
    for d in range(cols):
        for j in range(CAP):
            c = got_ref[nxt * cols + d, j]
            for k in range(knz):
                info_ref[d * CAP + j, k] = slot_ref[c, k]


def feature_kernel(cols, blk, got_ref, feat_ref, out_ref):
    batches, rows, _ = feat_ref.shape
    half = batches // CORES
    for z in range(cols // CORES):
        for cd in range(CORES):
            for j in range(CAP):
                b = got_ref[z * CORES + cd, j]
                x = feat_ref[:, :, pl.ds(pl.multiple_of(b * blk, blk), blk)].astype(jnp.float32)
                x = x.reshape(batches * rows, blk).astype(jnp.bfloat16)
                for cp in range(CORES):
                    out_ref[z * CORES + cp, cd * CAP + j] = x[cp * half * rows : (cp + 1) * half * rows]


def weight_kernel(got_ref, w_ref, b_ref, wo_ref, bo_ref):
    wo_ref[...] = w_ref[...]
    bo_ref[...] = b_ref[...]


def run_layer(zs, blk, pool, infos, ws, bs, outs):
    z = lax.axis_index("col") // CORES
    knz = infos[0].shape[1]
    for dz in range(zs):
        zd = lax.rem(z + dz, zs)
        for cd in range(CORES):
            for cc in range(CORES):
                for j in range(CAP):
                    i = (zd * CORES + cd) * CAP + j
                    x = jnp.concatenate(
                        [pool[cc * (zs * CORES * CAP) + infos[cc][i, k]] for k in range(knz)], axis=1
                    )
                    y = jnp.dot(x, ws[cc][i], preferred_element_type=jnp.float32) + bs[cc][i]
                    outs[dz][cd * (CORES * CAP) + cc * CAP + j] = jnp.clip(y, 0.0, 32.0).astype(jnp.bfloat16)


def first_kernel(sections, zs, blk, recv_ref, io, js, wo, ws, bo, bs, *rest):
    outs, pool = rest[:-1], rest[-1]
    part = recv_ref.shape[2]
    cols = zs * CORES
    core = lax.rem(lax.axis_index("col"), CORES)
    for s in range(sections):
        for e in range(cols):
            for cd in range(CORES):
                for j in range(CAP):
                    pool[cd * cols * CAP + e * CAP + j, s * part : (s + 1) * part] = recv_ref[s * cols + e, cd * CAP + j]
    pair(core, zs, blk, pool, io, js, wo, ws, bo, bs, outs)


def pair(core, zs, blk, pool, io, js, wo, ws, bo, bs, outs):
    @pl.when(core == 0)
    def _():
        run_layer(zs, blk, pool, (io, js), (wo, ws), (bo, bs), outs)

    @pl.when(core != 0)
    def _():
        run_layer(zs, blk, pool, (js, io), (ws, wo), (bs, bo), outs)


def middle_kernel(zs, blk, *refs):
    ins, (io, js, wo, ws, bo, bs), outs, pool = refs[:zs], refs[zs : zs + 6], refs[zs + 6 : -1], refs[-1]
    cols = zs * CORES
    z = lax.axis_index("col") // CORES
    core = lax.rem(lax.axis_index("col"), CORES)
    per = CORES * CAP
    for dz in range(zs):
        ze = lax.rem(z - dz + zs, zs)
        for cd in range(CORES):
            for q in range(per):
                pool[cd * cols * CAP + ze * per + q] = ins[dz][cd * per + q]
    pair(core, zs, blk, pool, io, js, wo, ws, bo, bs, outs)


def last_kernel(zs, sections, rows_own, *refs):
    ins, sib, slot, rows_ref, w_ref, b_ref = refs[:zs], *refs[zs : zs + 5]
    outs, pool = refs[zs + 5 : -1], refs[-1]
    g = pl.program_id(0)
    col = lax.axis_index("col")
    z, core = col // CORES, lax.rem(col, CORES)
    per = CORES * CAP
    half = ins[0].shape[1]
    blk = ins[0].shape[2]
    part = half // sections
    batches = outs[0].shape[0]

    @pl.when(g == 0)
    def _():
        mine = pl.ds(pl.multiple_of(core * half, half), half)
        other = pl.ds(pl.multiple_of((1 - core) * half, half), half)
        for dz in range(zs):
            ze = lax.rem(z - dz + zs, zs)
            for q in range(per):
                pool[ze * per + q, mine, :] = ins[dz][core * per + q]
                pool[ze * per + q, other, :] = sib[dz, q]

    columns, knz = w_ref.shape[0], slot.shape[1]
    ids = lax.broadcasted_iota(jnp.int32, (rows_own, 1), 0)
    live = []
    for s in range(sections):
        live.append([(s * rows_own + ids) < rows_ref[m] for m in range(batches)])
    for n in range(columns):
        c = g * columns + n
        x = jnp.concatenate([pool[slot[c, k]] for k in range(knz)], axis=1)
        y = jnp.dot(x, w_ref[n], preferred_element_type=jnp.float32) + b_ref[:, n * blk : (n + 1) * blk]
        y = jnp.clip(y, 0.0, 32.0)
        for s in range(sections):
            for m in range(batches):
                h, mp = m // (batches // CORES), m % (batches // CORES)
                at = h * half + s * part + mp * rows_own
                t = jnp.where(live[s][m], y[at : at + rows_own], 0.0)
                outs[s][m, :, n * blk : (n + 1) * blk] = t.astype(jnp.bfloat16)


def body(features, weights, sources, bias, batch_rows):
    sections = lax.axis_size("section")
    cols = lax.axis_size("col")
    zs = cols // CORES
    w = weights[0]
    blocks_own, knz, blk, _ = w.shape
    batches, rows_own, _ = features.shape
    need = cols * CAP
    half = batches * rows_own * sections // CORES
    part = half // sections
    bf, i32, f32 = jnp.bfloat16, jnp.int32, jnp.float32
    S = jax.ShapeDtypeStruct
    section = lax.axis_index("section")

    ask, slot = pl.pallas_call(
        functools.partial(pool_kernel, cols, blocks_own),
        out_shape=(S((sections * cols, CAP), i32), S((blocks_own, knz), i32)),
        in_specs=[VM],
        out_specs=(VM, VM),
        name="pools",
    )(sources[0])
    got = lax.all_to_all(ask, BOTH, 0, 0, tiled=True)

    sends = pl.pallas_call(
        functools.partial(feature_kernel, cols, blk),
        out_shape=S((sections * cols, CORES * CAP, part, blk), bf),
        in_specs=[SM, VM],
        out_specs=VM,
        name="gather_features",
    )(got, features)
    recv = lax.all_to_all(sends, BOTH, 0, 0, tiled=True)

    info = pl.pallas_call(
        functools.partial(need_kernel, sections, cols, knz),
        out_shape=S((need, knz), i32),
        in_specs=[SM, SM],
        out_specs=SM,
        name="needs",
    )(got, slot)

    def wanted(i, got_ref):
        nxt = jnp.minimum(lax.axis_index("section") + 1, sections - 1)
        return got_ref[nxt * cols + i // CAP, lax.rem(i, CAP)]

    wn, bn = pl.pallas_call(
        weight_kernel,
        grid_spec=pltpu.PrefetchScalarGridSpec(
            num_scalar_prefetch=1,
            grid=(need,),
            in_specs=[
                pl.BlockSpec((1, knz * blk, blk), lambda i, g: (wanted(i, g), 0, 0)),
                pl.BlockSpec((1, 1, blk), lambda i, g: (wanted(i, g), 0, 0)),
            ],
            out_specs=[
                pl.BlockSpec((1, knz * blk, blk), lambda i, g: (i, 0, 0)),
                pl.BlockSpec((1, 1, blk), lambda i, g: (i, 0, 0)),
            ],
        ),
        out_shape=(S((need, knz * blk, blk), bf), S((need, 1, blk), f32)),
        name="gather_weights",
    )(got, w.reshape(blocks_own, knz * blk, blk), bias[0].reshape(blocks_own, 1, blk))

    total = sections * cols
    sibling = [(i, i ^ 1) for i in range(total)]
    ws = lax.ppermute(wn, BOTH, sibling)
    bs = lax.ppermute(bn, BOTH, sibling)
    js = lax.ppermute(info, BOTH, sibling)

    layer_args = (info, js, wn, ws, bn, bs)
    layer_specs = [SM, SM, VM, VM, VM, VM]
    piece = S((CORES * CORES * CAP, half, blk), bf)
    scratch = [pltpu.VMEM((CORES * need, half, blk), bf)]
    params = pltpu.CompilerParams(vmem_limit_bytes=24 << 20)

    def shift(xs, layer):
        def pairs(dz):
            return [(layer * cols + e, (layer + 1) * cols + (e + CORES * dz) % cols) for e in range(cols)]

        return [lax.ppermute(x, BOTH, pairs(dz)) for dz, x in enumerate(xs)]

    xs = pl.pallas_call(
        functools.partial(first_kernel, sections, zs, blk),
        out_shape=(piece,) * zs,
        in_specs=[VM] + layer_specs,
        out_specs=(VM,) * zs,
        scratch_shapes=scratch,
        compiler_params=params,
        name="first_layer",
    )(recv, *layer_args)
    xs = shift(xs, 0)
    for layer in range(1, sections - 1):
        xs = pl.pallas_call(
            functools.partial(middle_kernel, zs, blk),
            out_shape=(piece,) * zs,
            in_specs=[VM] * zs + layer_specs,
            out_specs=(VM,) * zs,
            scratch_shapes=scratch,
            compiler_params=params,
            name="middle_layer",
        )(*xs, *layer_args)
        xs = shift(xs, layer)

    core = lax.rem(lax.axis_index("col"), CORES)
    per = CORES * CAP
    give = jnp.stack([lax.dynamic_slice_in_dim(x, (1 - core) * per, per, 0) for x in xs])
    sib = lax.ppermute(give, BOTH, sibling)

    steps = 8
    columns = blocks_own // steps
    outs = pl.pallas_call(
        functools.partial(last_kernel, zs, sections, rows_own),
        grid=(steps,),
        out_shape=(S((batches, rows_own, blocks_own * blk), bf),) * sections,
        in_specs=[VM] * (zs + 1)
        + [
            SM,
            SM,
            pl.BlockSpec((columns, knz * blk, blk), lambda g: (g, 0, 0)),
            pl.BlockSpec((1, columns * blk), lambda g: (0, g)),
        ],
        out_specs=(pl.BlockSpec((batches, rows_own, columns * blk), lambda g: (0, 0, g)),) * sections,
        scratch_shapes=[pltpu.VMEM((need, half * CORES, blk), bf)],
        compiler_params=params,
        name="last_layer",
    )(*xs, sib, slot, batch_rows, w.reshape(blocks_own, knz * blk, blk), bias)

    result = outs[-1]
    for s in range(sections - 1):
        there = lax.ppermute(outs[s], BOTH, [((sections - 1) * cols + e, s * cols + e) for e in range(cols)])
        result = jnp.where(section == s, there, result)
    return result


def solution(mesh):
    in_specs = (
        P(None, "section", "col"),
        P("section", "col", None, None, None),
        P("section", "col", None),
        P("section", "col"),
        P(),
    )
    out_specs = P(None, "section", "col")
    return jax.shard_map(body, mesh=mesh, in_specs=in_specs, out_specs=out_specs, check_vma=False)
```

```python
import functools

import jax
import jax.numpy as jnp
from jax import lax
from jax.experimental import pallas as pl
from jax.experimental.pallas import tpu as pltpu
from jax.sharding import PartitionSpec as P

CAP = 2
CORES = 2
BOTH = ("section", "col")
VM = pl.BlockSpec(memory_space=pltpu.VMEM)
SM = pl.BlockSpec(memory_space=pltpu.SMEM)
HB = pl.BlockSpec(memory_space=pl.ANY)
BIG = 1 << 30


def pool_kernel(cols, blocks_own, src_ref, ask_ref, slot_ref):
    src = src_ref[...]
    owner = src // blocks_own
    slot = jnp.zeros_like(src)
    lows, highs = [], []
    for e in range(cols):
        mine = owner == e
        low = jnp.min(jnp.where(mine, src, BIG), axis=(0, 1), keepdims=True)
        high = jnp.max(jnp.where(mine, src, -1), axis=(0, 1), keepdims=True)
        slot = jnp.where(mine, CAP * e + (src > low).astype(jnp.int32), slot)
        lows.append(low - e * blocks_own)
        highs.append(high - e * blocks_own)
    slot_ref[...] = slot
    for e in range(cols):
        o = e ^ 1
        both = jnp.concatenate([lows[e], highs[e], lows[o], highs[o]], axis=1)
        for s in range(ask_ref.shape[0] // cols):
            ask_ref[s * cols + e] = both


def prepare_kernel(sections, cols, got_ref, slot_ref, sib_slot_ref, w_ref, b_ref, sb_ref, wo_ref, bo_ref, info_ref, sem):
    nxt = jnp.minimum(lax.axis_index("section") + 1, sections - 1)
    need = cols * CAP
    copies = []
    for i in range(need):
        c = got_ref[nxt * cols + i // CAP, 0, i % CAP]
        copies.append(pltpu.make_async_copy(w_ref.at[c], wo_ref.at[i], sem.at[i]))
        copies[-1].start()
    for r, (slots, src) in enumerate(((slot_ref, b_ref), (sib_slot_ref, sb_ref))):
        for i in range(need):
            c = got_ref[nxt * cols + i // CAP, 0, r * CAP + i % CAP]
            bo_ref[r * need + i] = src[c]
            for k in range(slots.shape[0]):
                info_ref[k, r * need + i] = slots[k, c]
            info_ref[slots.shape[0], r * need + i] = c
    for copy in copies:
        copy.wait()


def resident_kernel(sections, w_ref, wv_ref, sem):
    @pl.when(lax.axis_index("section") == sections - 1)
    def _():
        copy = pltpu.make_async_copy(w_ref, wv_ref, sem)
        copy.start()
        copy.wait()


def feature_kernel(cols, got_ref, feat_ref, out_ref):
    blk = out_ref.shape[4]
    half = out_ref.shape[2]
    for z in range(cols // CORES):
        for cd in range(CORES):
            for j in range(CAP):
                b = got_ref[z * CORES + cd, 0, j]
                at = pl.ds(pl.multiple_of(b * blk, blk), blk)
                for cp in range(CORES):
                    out_ref[z * CORES + cp, cd * CAP + j] = feat_ref[cp * half : (cp + 1) * half, :, at]


def run_layer(zs, blk, core, rel, pool, w, b, info, outs):
    z = lax.axis_index("col") // CORES
    knz = info.shape[0] - 1
    need = zs * CORES * CAP
    cc = lax.rem(core + rel, CORES)
    for dz in range(zs):
        zd = lax.rem(z + dz, zs)
        for cd in range(CORES):
            for j in range(CAP):
                i = (zd * CORES + cd) * CAP + j
                at = rel * need + i
                x = jnp.concatenate([pool[cc * need + info[k, at]] for k in range(knz)], axis=1)
                y = jnp.dot(x, w[i], preferred_element_type=jnp.float32) + b[at]
                outs[dz][cd * (CORES * CAP) + cc * CAP + j] = jnp.clip(y, 0.0, 32.0).astype(jnp.bfloat16)


def first_kernel(sections, zs, blk, recv_ref, w, b, info, sw_ref, *rest):
    outs, ws, pool, sem = rest[:zs], rest[zs], rest[zs + 1], rest[zs + 2]
    part = recv_ref.shape[2]
    cols = zs * CORES
    need = cols * CAP
    core = lax.rem(lax.axis_index("col"), CORES)
    here = lax.axis_index("section") == 0
    copies = []
    for i in range(need):
        copies.append(pltpu.make_async_copy(sw_ref.at[info[info.shape[0] - 1, need + i]], ws.at[i], sem.at[i]))
        copies[-1].start()

    @pl.when(here)
    def _():
        for s in range(sections):
            for e in range(cols):
                for cd in range(CORES):
                    for j in range(CAP):
                        pool[cd * need + e * CAP + j, s * part : (s + 1) * part] = recv_ref[s * cols + e, cd * CAP + j]
        run_layer(zs, blk, core, 0, pool, w, b, info, outs)

    for copy in copies:
        copy.wait()

    @pl.when(here)
    def _():
        run_layer(zs, blk, core, 1, pool, ws, b, info, outs)


def middle_kernel(zs, blk, layer, *refs):
    ins, (w, b, info, ws), outs, pool = refs[:zs], refs[zs : zs + 4], refs[zs + 4 : -1], refs[-1]
    cols = zs * CORES
    z = lax.axis_index("col") // CORES
    core = lax.rem(lax.axis_index("col"), CORES)
    per = CORES * CAP

    @pl.when(lax.axis_index("section") == layer)
    def _():
        for dz in range(zs):
            ze = lax.rem(z - dz + zs, zs)
            for cd in range(CORES):
                for q in range(per):
                    pool[cd * cols * CAP + ze * per + q] = ins[dz][cd * per + q]
        run_layer(zs, blk, core, 0, pool, w, b, info, outs)
        run_layer(zs, blk, core, 1, pool, ws, b, info, outs)


def last_kernel(zs, sections, rows_own, relays, *refs):
    @pl.when(lax.axis_index("section") == sections - 1)
    def _():
        last_layer(zs, sections, rows_own, relays, *refs)


def last_layer(zs, sections, rows_own, relays, *refs):
    ins, sib, slot, rows_ref, w_ref, b_ref = refs[:zs], *refs[zs : zs + 5]
    outs, pool = refs[zs + 5 : -1], refs[-1]
    col = lax.axis_index("col")
    z, core = col // CORES, lax.rem(col, CORES)
    per = CORES * CAP
    half = ins[0].shape[1]
    blk = ins[0].shape[2]
    part = half // sections
    batches = rows_ref.shape[0]
    mine = pl.ds(pl.multiple_of(core * half, half), half)
    other = pl.ds(pl.multiple_of((1 - core) * half, half), half)
    for dz in range(zs):
        ze = lax.rem(z - dz + zs, zs)
        for q in range(per):
            pool[ze * per + q, mine, :] = ins[dz][core * per + q]
            pool[ze * per + q, other, :] = sib[dz, q]

    columns, knz = w_ref.shape[0], slot.shape[0]
    ids = lax.broadcasted_iota(jnp.int32, (rows_own, 1), 0)
    live = []
    for s in range(sections):
        live.append([(s * rows_own + ids) < rows_ref[m] for m in range(batches)])
    place = {}
    n_out = 0
    for s in range(sections):
        if s in relays:
            for m in range(batches):
                place[s, m] = (n_out + m // (batches // 2), m % (batches // 2))
            n_out += 2
        else:
            for m in range(batches):
                place[s, m] = (n_out, m)
            n_out += 1
    for c in range(columns):
        x = jnp.concatenate([pool[slot[k, c]] for k in range(knz)], axis=1)
        y = jnp.dot(x, w_ref[c], preferred_element_type=jnp.float32) + b_ref[:, c * blk : (c + 1) * blk]
        y = jnp.clip(y, 0.0, 32.0)
        for s in range(sections):
            for m in range(batches):
                h, mp = m // (batches // CORES), m % (batches // CORES)
                at = h * half + s * part + mp * rows_own
                t = jnp.where(live[s][m], y[at : at + rows_own], 0.0)
                o, mm = place[s, m]
                outs[o][mm, :, c * blk : (c + 1) * blk] = t.astype(jnp.bfloat16)


def body(features, weights, sources, bias, batch_rows):
    sections = lax.axis_size("section")
    cols = lax.axis_size("col")
    zs = cols // CORES
    w = weights[0]
    blocks_own, knz, blk, _ = w.shape
    batches, rows_own, _ = features.shape
    need = cols * CAP
    half = batches * rows_own * sections // CORES
    part = half // sections
    bf, i32, f32 = jnp.bfloat16, jnp.int32, jnp.float32
    S = jax.ShapeDtypeStruct
    section = lax.axis_index("section")

    def room(mib):
        return pltpu.CompilerParams(vmem_limit_bytes=mib << 20)

    ask, slot = pl.pallas_call(
        functools.partial(pool_kernel, cols, blocks_own),
        out_shape=(S((sections * cols, 1, CORES * CAP), i32), S((knz, blocks_own), i32)),
        in_specs=[VM],
        out_specs=(VM, VM),
        compiler_params=room(46),
        name="pools",
    )(sources[0].T)
    got = lax.all_to_all(ask, BOTH, 0, 0, tiled=True)

    total = sections * cols
    sibling = [(i, i ^ 1) for i in range(total)]
    w3 = w.reshape(blocks_own, knz * blk, blk)
    b3 = bias[0].reshape(blocks_own, 1, blk)
    w_then, _ = lax.optimization_barrier((w3, got))
    sw3 = lax.ppermute(w_then, BOTH, sibling)
    sb3 = lax.ppermute(b3, BOTH, sibling)
    sib_slot = lax.ppermute(slot, BOTH, sibling)

    sends = pl.pallas_call(
        functools.partial(feature_kernel, cols),
        out_shape=S((sections * cols, CORES * CAP, batches // CORES, rows_own, blk), bf),
        in_specs=[SM, VM],
        out_specs=VM,
        compiler_params=room(56),
        name="gather_features",
    )(got, features)
    recv = lax.all_to_all(sends.reshape(sections * cols, CORES * CAP, part, blk), BOTH, 0, 0, tiled=True)

    layer_args = pl.pallas_call(
        functools.partial(prepare_kernel, sections, cols),
        out_shape=(S((need, knz * blk, blk), bf), S((CORES * need, 1, blk), f32), S((knz + 1, CORES * need), i32)),
        in_specs=[SM, SM, SM, HB, VM, VM],
        out_specs=(VM, VM, SM),
        scratch_shapes=[pltpu.SemaphoreType.DMA((need,))],
        compiler_params=room(46),
        name="prepare",
    )(got, slot, sib_slot, w3, b3, sb3)
    layer_specs = [VM, VM, SM]
    piece = S((CORES * CORES * CAP, half, blk), bf)
    scratch = [pltpu.VMEM((CORES * need, half, blk), bf)]
    params = room(24)

    def shift(xs, layer):
        def pairs(dz):
            return [(layer * cols + e, (layer + 1) * cols + (e + CORES * dz) % cols) for e in range(cols)]

        order = sorted(range(zs), key=lambda dz: -min(dz, zs - dz))
        ys = {dz: lax.ppermute(xs[dz], BOTH, pairs(dz)) for dz in order}
        return [ys[dz] for dz in range(zs)]

    *xs, ws = pl.pallas_call(
        functools.partial(first_kernel, sections, zs, blk),
        out_shape=(piece,) * zs + (S((need, knz * blk, blk), bf),),
        in_specs=[VM] + layer_specs + [HB],
        out_specs=(VM,) * (zs + 1),
        scratch_shapes=scratch + [pltpu.SemaphoreType.DMA((need,))],
        compiler_params=room(44),
        name="first_layer",
    )(recv, *layer_args, sw3)
    xs = shift(xs, 0)
    for layer in range(1, sections - 1):
        xs = pl.pallas_call(
            functools.partial(middle_kernel, zs, blk, layer),
            out_shape=(piece,) * zs,
            in_specs=[VM] * zs + layer_specs + [VM],
            out_specs=(VM,) * zs,
            scratch_shapes=scratch,
            compiler_params=params,
            name="middle_layer",
        )(*xs, *layer_args, ws)
        xs = shift(xs, layer)

    w_late, xs[0] = lax.optimization_barrier((w3, xs[0]))
    wv = pl.pallas_call(
        functools.partial(resident_kernel, sections),
        out_shape=S(w3.shape, bf),
        in_specs=[HB],
        out_specs=VM,
        scratch_shapes=[pltpu.SemaphoreType.DMA],
        cost_estimate=pl.CostEstimate(flops=0, bytes_accessed=w3.size * 4, transcendentals=0),
        compiler_params=room(40),
        name="resident_weights",
    )(w_late)
    *xs[1:], wv = lax.optimization_barrier((*xs[1:], wv))

    core = lax.rem(lax.axis_index("col"), CORES)
    per = CORES * CAP
    give = jnp.stack([lax.dynamic_slice_in_dim(x, (1 - core) * per, per, 0) for x in xs])
    sib = lax.ppermute(give, BOTH, sibling)

    relays = {0: 1} if sections == 4 and batches % 2 == 0 else {}
    last = sections - 1
    shapes = []
    for s in range(sections):
        shapes += [(batches // 2, rows_own, blocks_own * blk)] * 2 if s in relays else [(batches, rows_own, blocks_own * blk)]
    outs = pl.pallas_call(
        functools.partial(last_kernel, zs, sections, rows_own, relays),
        out_shape=tuple(S(shape, bf) for shape in shapes),
        in_specs=[VM] * (zs + 1) + [SM, SM, VM, VM],
        out_specs=(VM,) * len(shapes),
        scratch_shapes=[pltpu.VMEM((need, half * CORES, blk), bf)],
        compiler_params=params,
        name="last_layer",
    )(*xs, sib, slot, batch_rows, wv, bias)

    def send(x, a, b):
        return lax.ppermute(x, BOTH, [(a * cols + e, b * cols + e) for e in range(cols)])

    outs = list(outs)
    there = {}
    for s in range(sections - 1):
        if s in relays:
            via = relays[s]
            hop = send(outs.pop(0), last, via)
            direct = send(outs.pop(0), last, s)
            there[s] = (hop, via, direct)
        else:
            there[s] = send(outs.pop(0), last, s)
    result = outs[-1]
    for s in range(sections - 1):
        if s in relays:
            hop, via, direct = there[s]
            there[s] = jnp.concatenate([send(hop, via, s), direct], axis=0)
        result = jnp.where(section == s, there[s], result)
    return result


def solution(mesh):
    in_specs = (
        P(None, "section", "col"),
        P("section", "col", None, None, None),
        P("section", "col", None),
        P("section", "col"),
        P(),
    )
    out_specs = P(None, "section", "col")
    return jax.shard_map(body, mesh=mesh, in_specs=in_specs, out_specs=out_specs, check_vma=False)
```

```python
import functools

import jax
import jax.numpy as jnp
from jax import lax
from jax.experimental import pallas as pl
from jax.experimental.pallas import tpu as pltpu
from jax.sharding import PartitionSpec as P

CAP = 2
CORES = 2
BOTH = ("section", "col")
VM = pl.BlockSpec(memory_space=pltpu.VMEM)
SM = pl.BlockSpec(memory_space=pltpu.SMEM)
HB = pl.BlockSpec(memory_space=pl.ANY)
BIG = 1 << 30


def pool_kernel(cols, blocks_own, src_ref, ask_ref, slot_ref):
    src = src_ref[...]
    owner = src // blocks_own
    slot = jnp.zeros_like(src)
    lows, highs = [], []
    for e in range(cols):
        mine = owner == e
        low = jnp.min(jnp.where(mine, src, BIG), axis=(0, 1), keepdims=True)
        high = jnp.max(jnp.where(mine, src, -1), axis=(0, 1), keepdims=True)
        slot = jnp.where(mine, CAP * e + (src > low).astype(jnp.int32), slot)
        lows.append(low - e * blocks_own)
        highs.append(high - e * blocks_own)
    slot_ref[...] = slot
    for e in range(cols):
        o = e ^ 1
        both = jnp.concatenate([lows[e], highs[e], lows[o], highs[o]], axis=1)
        for s in range(ask_ref.shape[0] // cols):
            ask_ref[s * cols + e] = both


def prepare_kernel(sections, cols, got_ref, slot_ref, sib_slot_ref, w_ref, b_ref, sb_ref, wo_ref, bo_ref, info_ref, sem):
    nxt = jnp.minimum(lax.axis_index("section") + 1, sections - 1)
    need = cols * CAP
    copies = []
    for i in range(need):
        c = got_ref[nxt * cols + i // CAP, 0, i % CAP]
        copies.append(pltpu.make_async_copy(w_ref.at[c], wo_ref.at[i], sem.at[i]))
        copies[-1].start()
    for r, (slots, src) in enumerate(((slot_ref, b_ref), (sib_slot_ref, sb_ref))):
        for i in range(need):
            c = got_ref[nxt * cols + i // CAP, 0, r * CAP + i % CAP]
            bo_ref[r * need + i] = src[c]
            for k in range(slots.shape[0]):
                info_ref[k, r * need + i] = slots[k, c]
            info_ref[slots.shape[0], r * need + i] = c
    for copy in copies:
        copy.wait()


def resident_kernel(sections, w_ref, wv_ref, sem):
    @pl.when(lax.axis_index("section") == sections - 1)
    def _():
        copy = pltpu.make_async_copy(w_ref, wv_ref, sem)
        copy.start()
        copy.wait()


def feature_kernel(cols, got_ref, feat_ref, out_ref):
    blk = out_ref.shape[4]
    half = out_ref.shape[2]
    for z in range(cols // CORES):
        for cd in range(CORES):
            for j in range(CAP):
                b = got_ref[z * CORES + cd, 0, j]
                at = pl.ds(pl.multiple_of(b * blk, blk), blk)
                for cp in range(CORES):
                    out_ref[z * CORES + cp, cd * CAP + j] = feat_ref[cp * half : (cp + 1) * half, :, at]


def run_layer(zs, blk, core, rel, pool, w, b, info, outs):
    z = lax.axis_index("col") // CORES
    knz = info.shape[0] - 1
    need = zs * CORES * CAP
    cc = lax.rem(core + rel, CORES)
    for dz in range(zs):
        zd = lax.rem(z + dz, zs)
        for cd in range(CORES):
            for j in range(CAP):
                i = (zd * CORES + cd) * CAP + j
                at = rel * need + i
                x = jnp.concatenate([pool[cc * need + info[k, at]] for k in range(knz)], axis=1)
                y = jnp.dot(x, w[i], preferred_element_type=jnp.float32) + b[at]
                outs[dz][cd * (CORES * CAP) + cc * CAP + j] = jnp.clip(y, 0.0, 32.0).astype(jnp.bfloat16)


def first_kernel(sections, zs, blk, recv_ref, w, b, info, sw_ref, *rest):
    outs, ws, pool, sem = rest[:zs], rest[zs], rest[zs + 1], rest[zs + 2]
    part = recv_ref.shape[2]
    cols = zs * CORES
    need = cols * CAP
    core = lax.rem(lax.axis_index("col"), CORES)
    here = lax.axis_index("section") == 0
    copies = []
    for i in range(need):
        copies.append(pltpu.make_async_copy(sw_ref.at[info[info.shape[0] - 1, need + i]], ws.at[i], sem.at[i]))
        copies[-1].start()

    @pl.when(here)
    def _():
        for s in range(sections):
            for e in range(cols):
                for cd in range(CORES):
                    for j in range(CAP):
                        pool[cd * need + e * CAP + j, s * part : (s + 1) * part] = recv_ref[s * cols + e, cd * CAP + j]
        run_layer(zs, blk, core, 0, pool, w, b, info, outs)

    for copy in copies:
        copy.wait()

    @pl.when(here)
    def _():
        run_layer(zs, blk, core, 1, pool, ws, b, info, outs)


def middle_kernel(zs, blk, layer, *refs):
    ins, (w, b, info, ws), outs, pool = refs[:zs], refs[zs : zs + 4], refs[zs + 4 : -1], refs[-1]
    cols = zs * CORES
    z = lax.axis_index("col") // CORES
    core = lax.rem(lax.axis_index("col"), CORES)
    per = CORES * CAP

    @pl.when(lax.axis_index("section") == layer)
    def _():
        for dz in range(zs):
            ze = lax.rem(z - dz + zs, zs)
            for cd in range(CORES):
                for q in range(per):
                    pool[cd * cols * CAP + ze * per + q] = ins[dz][cd * per + q]
        run_layer(zs, blk, core, 0, pool, w, b, info, outs)
        run_layer(zs, blk, core, 1, pool, ws, b, info, outs)


def last_kernel(zs, sections, rows_own, mine, first, *refs):
    @pl.when(lax.axis_index("section") == sections - 1)
    def _():
        last_layer(zs, sections, rows_own, mine, first, *refs)


def last_layer(zs, sections, rows_own, mine, first, *refs):
    if first:
        ins, sib, refs = refs[:zs], refs[zs], refs[zs + 1 :]
        slot, rows_ref, w_ref, b_ref, *outs, pool = refs
    else:
        pool, slot, rows_ref, w_ref, b_ref, *outs = refs
    col = lax.axis_index("col")
    z, core = col // CORES, lax.rem(col, CORES)
    per = CORES * CAP
    blk = pool.shape[3]
    batches = rows_ref.shape[0]
    part = pool.shape[2] // CORES
    if first:
        for dz in range(zs):
            ze = lax.rem(z - dz + zs, zs)
            for q in range(per):
                for s in range(sections):
                    rows = slice(s * part, (s + 1) * part)
                    own, other = ins[dz][core * per + q, rows], sib[dz, q, rows]
                    for h in range(CORES):
                        pool[s, ze * per + q, h * part : (h + 1) * part] = jnp.where(core == h, own, other)

    columns, knz = w_ref.shape[0], slot.shape[0]
    ids = lax.broadcasted_iota(jnp.int32, (rows_own, 1), 0)
    live = {s: [(s * rows_own + ids) < rows_ref[m] for m in range(batches)] for s, _ in mine}
    for c in range(columns):
        x = jnp.concatenate(
            [
                jnp.concatenate([pool[s, slot[k, c]] for k in range(knz)], axis=1)
                for s, _ in mine
            ],
            axis=0,
        )
        y = jnp.dot(x, w_ref[c], preferred_element_type=jnp.float32) + b_ref[:, c * blk : (c + 1) * blk]
        y = jnp.clip(y, 0.0, 32.0)
        out = 0
        for n, (s, cuts) in enumerate(mine):
            for m in range(batches):
                at = n * CORES * part + m * rows_own
                t = jnp.where(live[s][m], y[at : at + rows_own], 0.0)
                o, mm = out + m // (batches // cuts), m % (batches // cuts)
                outs[o][mm, :, c * blk : (c + 1) * blk] = t.astype(jnp.bfloat16)
            out += cuts


def body(features, weights, sources, bias, batch_rows):
    sections = lax.axis_size("section")
    cols = lax.axis_size("col")
    zs = cols // CORES
    w = weights[0]
    blocks_own, knz, blk, _ = w.shape
    batches, rows_own, _ = features.shape
    need = cols * CAP
    half = batches * rows_own * sections // CORES
    part = half // sections
    bf, i32, f32 = jnp.bfloat16, jnp.int32, jnp.float32
    S = jax.ShapeDtypeStruct
    section = lax.axis_index("section")

    def room(mib):
        return pltpu.CompilerParams(vmem_limit_bytes=mib << 20)

    ask, slot = pl.pallas_call(
        functools.partial(pool_kernel, cols, blocks_own),
        out_shape=(S((sections * cols, 1, CORES * CAP), i32), S((knz, blocks_own), i32)),
        in_specs=[VM],
        out_specs=(VM, VM),
        compiler_params=room(46),
        name="pools",
    )(sources[0].T)
    got = lax.all_to_all(ask, BOTH, 0, 0, tiled=True)

    total = sections * cols
    sibling = [(i, i ^ 1) for i in range(total)]
    w3 = w.reshape(blocks_own, knz * blk, blk)
    b3 = bias[0].reshape(blocks_own, 1, blk)
    w_then, _ = lax.optimization_barrier((w3, got))
    sw3 = lax.ppermute(w_then, BOTH, sibling)
    sb3 = lax.ppermute(b3, BOTH, sibling)
    sib_slot = lax.ppermute(slot, BOTH, sibling)

    sends = pl.pallas_call(
        functools.partial(feature_kernel, cols),
        out_shape=S((sections * cols, CORES * CAP, batches // CORES, rows_own, blk), bf),
        in_specs=[SM, VM],
        out_specs=VM,
        compiler_params=room(56),
        name="gather_features",
    )(got, features)
    recv = lax.all_to_all(sends.reshape(sections * cols, CORES * CAP, part, blk), BOTH, 0, 0, tiled=True)

    layer_args = pl.pallas_call(
        functools.partial(prepare_kernel, sections, cols),
        out_shape=(S((need, knz * blk, blk), bf), S((CORES * need, 1, blk), f32), S((knz + 1, CORES * need), i32)),
        in_specs=[SM, SM, SM, HB, VM, VM],
        out_specs=(VM, VM, SM),
        scratch_shapes=[pltpu.SemaphoreType.DMA((need,))],
        compiler_params=room(46),
        name="prepare",
    )(got, slot, sib_slot, w3, b3, sb3)
    layer_specs = [VM, VM, SM]
    piece = S((CORES * CORES * CAP, half, blk), bf)
    scratch = [pltpu.VMEM((CORES * need, half, blk), bf)]
    params = room(24)

    def shift(xs, layer):
        def pairs(dz):
            return [(layer * cols + e, (layer + 1) * cols + (e + CORES * dz) % cols) for e in range(cols)]

        order = sorted(range(zs), key=lambda dz: -min(dz, zs - dz))
        ys = {dz: lax.ppermute(xs[dz], BOTH, pairs(dz)) for dz in order}
        return [ys[dz] for dz in range(zs)]

    *xs, ws = pl.pallas_call(
        functools.partial(first_kernel, sections, zs, blk),
        out_shape=(piece,) * zs + (S((need, knz * blk, blk), bf),),
        in_specs=[VM] + layer_specs + [HB],
        out_specs=(VM,) * (zs + 1),
        scratch_shapes=scratch + [pltpu.SemaphoreType.DMA((need,))],
        compiler_params=room(44),
        name="first_layer",
    )(recv, *layer_args, sw3)
    xs = shift(xs, 0)
    for layer in range(1, sections - 1):
        xs = pl.pallas_call(
            functools.partial(middle_kernel, zs, blk, layer),
            out_shape=(piece,) * zs,
            in_specs=[VM] * zs + layer_specs + [VM],
            out_specs=(VM,) * zs,
            scratch_shapes=scratch,
            compiler_params=params,
            name="middle_layer",
        )(*xs, *layer_args, ws)
        xs = shift(xs, layer)

    w_late, xs[0] = lax.optimization_barrier((w3, xs[0]))
    wv = pl.pallas_call(
        functools.partial(resident_kernel, sections),
        out_shape=S(w3.shape, bf),
        in_specs=[HB],
        out_specs=VM,
        scratch_shapes=[pltpu.SemaphoreType.DMA],
        cost_estimate=pl.CostEstimate(flops=0, bytes_accessed=w3.size * 4, transcendentals=0),
        compiler_params=room(40),
        name="resident_weights",
    )(w_late)
    *xs[1:], wv = lax.optimization_barrier((*xs[1:], wv))

    core = lax.rem(lax.axis_index("col"), CORES)
    per = CORES * CAP
    give = jnp.stack([lax.dynamic_slice_in_dim(x, (1 - core) * per, per, 0) for x in xs])
    sib = lax.ppermute(give, BOTH, sibling)

    relays = {0: 1} if sections == 4 and batches % 2 == 0 else {}
    last = sections - 1
    per_section = half * CORES // sections

    def last_call(mine, first, operands, name):
        shapes = [
            S((batches // cuts, rows_own, blocks_own * blk), bf) for _, cuts in mine for _ in range(cuts)
        ]
        if first:
            shapes.append(S((sections, need, per_section, blk), bf))
        return pl.pallas_call(
            functools.partial(last_kernel, zs, sections, rows_own, mine, first),
            out_shape=tuple(shapes),
            in_specs=[VM] * (len(operands) - 4) + [SM, SM, VM, VM],
            out_specs=(VM,) * len(shapes),
            compiler_params=params,
            name=name,
        )(*operands)

    mine = [(s, 2 if s in relays else 1) for s in range(sections)]
    *outs, pool = last_call(mine[:1], True, (*xs, sib, slot, batch_rows, wv, bias), "last_layer")
    outs += last_call(mine[1:], False, (pool, slot, batch_rows, wv, bias), "last_layer_rest")

    def send(x, a, b):
        return lax.ppermute(x, BOTH, [(a * cols + e, b * cols + e) for e in range(cols)])

    there = {}
    for s in range(sections - 1):
        if s in relays:
            via = relays[s]
            hop = send(outs.pop(0), last, via)
            direct = send(outs.pop(0), last, s)
            there[s] = (hop, via, direct)
        else:
            there[s] = send(outs.pop(0), last, s)
    result = outs[-1]
    for s in range(sections - 1):
        if s in relays:
            hop, via, direct = there[s]
            hop, direct = lax.optimization_barrier((hop, direct))
            there[s] = jnp.concatenate([send(hop, via, s), direct], axis=0)
        result = jnp.where(section == s, there[s], result)
    return result


def solution(mesh):
    in_specs = (
        P(None, "section", "col"),
        P("section", "col", None, None, None),
        P("section", "col", None),
        P("section", "col"),
        P(),
    )
    out_specs = P(None, "section", "col")
    return jax.shard_map(body, mesh=mesh, in_specs=in_specs, out_specs=out_specs, check_vma=False)
```

```python
import functools

import jax
import jax.numpy as jnp
from jax import lax
from jax.experimental import pallas as pl
from jax.experimental.pallas import tpu as pltpu
from jax.sharding import PartitionSpec as P

CAP = 2
CORES = 2
BOTH = ("section", "col")
VM = pl.BlockSpec(memory_space=pltpu.VMEM)
SM = pl.BlockSpec(memory_space=pltpu.SMEM)
HB = pl.BlockSpec(memory_space=pl.ANY)
BIG = 1 << 30


def pool_kernel(cols, blocks_own, src_ref, ask_ref, slot_ref):
    src = src_ref[...]
    owner = src // blocks_own
    slot = jnp.zeros_like(src)
    lows, highs = [], []
    for e in range(cols):
        mine = owner == e
        low = jnp.min(jnp.where(mine, src, BIG), axis=(0, 1), keepdims=True)
        high = jnp.max(jnp.where(mine, src, -1), axis=(0, 1), keepdims=True)
        slot = jnp.where(mine, CAP * e + (src > low).astype(jnp.int32), slot)
        lows.append(low - e * blocks_own)
        highs.append(high - e * blocks_own)
    slot_ref[...] = slot
    for e in range(cols):
        o = e ^ 1
        both = jnp.concatenate([lows[e], highs[e], lows[o], highs[o]], axis=1)
        for s in range(ask_ref.shape[0] // cols):
            ask_ref[s * cols + e] = both


def prepare_kernel(sections, cols, got_ref, slot_ref, sib_slot_ref, w_ref, b_ref, sb_ref, wo_ref, bo_ref, info_ref, sem):
    nxt = jnp.minimum(lax.axis_index("section") + 1, sections - 1)
    need = cols * CAP
    copies = []
    for i in range(need):
        c = got_ref[nxt * cols + i // CAP, 0, i % CAP]
        copies.append(pltpu.make_async_copy(w_ref.at[c], wo_ref.at[i], sem.at[i]))
        copies[-1].start()
    for r, (slots, src) in enumerate(((slot_ref, b_ref), (sib_slot_ref, sb_ref))):
        for i in range(need):
            c = got_ref[nxt * cols + i // CAP, 0, r * CAP + i % CAP]
            bo_ref[r * need + i] = src[c]
            for k in range(slots.shape[0]):
                info_ref[k, r * need + i] = slots[k, c]
            info_ref[slots.shape[0], r * need + i] = c
    for copy in copies:
        copy.wait()


def resident_kernel(sections, w_ref, wv_ref, sem):
    @pl.when(lax.axis_index("section") == sections - 1)
    def _():
        copy = pltpu.make_async_copy(w_ref, wv_ref, sem)
        copy.start()
        copy.wait()


def feature_kernel(cols, got_ref, feat_ref, out_ref, near, sem):
    blk = near.shape[4]
    half = near.shape[2]
    for z in range(cols // CORES):
        for cd in range(CORES):
            for j in range(CAP):
                b = got_ref[z * CORES + cd, 0, j]
                at = pl.ds(pl.multiple_of(b * blk, blk), blk)
                for cp in range(CORES):
                    near[z * CORES + cp, cd * CAP + j] = feat_ref[cp * half : (cp + 1) * half, :, at]
    copy = pltpu.make_async_copy(near, out_ref.at[pl.ds(0, cols)], sem)
    copy.start()
    copy.wait()


def run_layer(zs, blk, core, rel, pool, w, b, info, outs):
    z = lax.axis_index("col") // CORES
    knz = info.shape[0] - 1
    need = zs * CORES * CAP
    cc = lax.rem(core + rel, CORES)
    for dz in range(zs):
        zd = lax.rem(z + dz, zs)
        for cd in range(CORES):
            for j in range(CAP):
                i = (zd * CORES + cd) * CAP + j
                at = rel * need + i
                x = jnp.concatenate([pool[cc * need + info[k, at]] for k in range(knz)], axis=1)
                y = jnp.dot(x, w[i], preferred_element_type=jnp.float32) + b[at]
                outs[dz][cd * (CORES * CAP) + cc * CAP + j] = jnp.clip(y, 0.0, 32.0).astype(jnp.bfloat16)


def first_kernel(sections, zs, blk, recv_ref, w, b, info, sw_ref, *rest):
    outs, ws, pool, sem = rest[:zs], rest[zs], rest[zs + 1], rest[zs + 2]
    part = recv_ref.shape[2]
    cols = zs * CORES
    need = cols * CAP
    core = lax.rem(lax.axis_index("col"), CORES)
    here = lax.axis_index("section") == 0
    copies = []
    for i in range(need):
        copies.append(pltpu.make_async_copy(sw_ref.at[info[info.shape[0] - 1, need + i]], ws.at[i], sem.at[i]))
        copies[-1].start()

    @pl.when(here)
    def _():
        for s in range(sections):
            for e in range(cols):
                for cd in range(CORES):
                    for j in range(CAP):
                        pool[cd * need + e * CAP + j, s * part : (s + 1) * part] = recv_ref[s * cols + e, cd * CAP + j]
        run_layer(zs, blk, core, 0, pool, w, b, info, outs)

    for copy in copies:
        copy.wait()

    @pl.when(here)
    def _():
        run_layer(zs, blk, core, 1, pool, ws, b, info, outs)


def take_kernel(x_ref, o_ref):
    o_ref[...] = x_ref[...]


def middle_kernel(zs, blk, layer, *refs):
    ins, (w, b, info, ws), outs, pool = refs[:zs], refs[zs : zs + 4], refs[zs + 4 : -1], refs[-1]
    cols = zs * CORES
    z = lax.axis_index("col") // CORES
    core = lax.rem(lax.axis_index("col"), CORES)
    per = CORES * CAP

    @pl.when(lax.axis_index("section") == layer)
    def _():
        for dz in range(zs):
            ze = lax.rem(z - dz + zs, zs)
            for cd in range(CORES):
                for q in range(per):
                    pool[cd * cols * CAP + ze * per + q] = ins[dz][cd * per + q]
        run_layer(zs, blk, core, 0, pool, w, b, info, outs)
        run_layer(zs, blk, core, 1, pool, ws, b, info, outs)


def last_kernel(zs, sections, rows_own, mine, first, *refs):
    @pl.when(lax.axis_index("section") == sections - 1)
    def _():
        last_layer(zs, sections, rows_own, mine, first, *refs)


def last_layer(zs, sections, rows_own, mine, first, *refs):
    if first:
        ins, sib, refs = refs[:zs], refs[zs], refs[zs + 1 :]
        slot, rows_ref, w_ref, b_ref, *outs, pool = refs
    else:
        pool, slot, rows_ref, w_ref, b_ref, *outs = refs
    col = lax.axis_index("col")
    z, core = col // CORES, lax.rem(col, CORES)
    per = CORES * CAP
    blk = pool.shape[3]
    batches = rows_ref.shape[0]
    part = pool.shape[2] // CORES
    if first:
        for dz in range(zs):
            ze = lax.rem(z - dz + zs, zs)
            for q in range(per):
                for s in range(sections):
                    rows = slice(s * part, (s + 1) * part)
                    own, other = ins[dz][core * per + q, rows], sib[dz, q, rows]
                    if part % 16 == 0:
                        pool[s, ze * per + q, pl.ds(pl.multiple_of(core * part, part), part), :] = own
                        pool[s, ze * per + q, pl.ds(pl.multiple_of((1 - core) * part, part), part), :] = other
                    else:
                        for h in range(CORES):
                            pool[s, ze * per + q, h * part : (h + 1) * part] = jnp.where(core == h, own, other)

    columns, knz = w_ref.shape[0], slot.shape[0]
    ids = lax.broadcasted_iota(jnp.int32, (rows_own, 1), 0)
    live = {s: [(s * rows_own + ids) < rows_ref[m] for m in range(batches)] for s, _ in mine}
    for c in range(columns):
        x = jnp.concatenate(
            [
                jnp.concatenate([pool[s, slot[k, c]] for k in range(knz)], axis=1)
                for s, _ in mine
            ],
            axis=0,
        )
        y = jnp.dot(x, w_ref[c], preferred_element_type=jnp.float32) + b_ref[:, c * blk : (c + 1) * blk]
        y = jnp.clip(y, 0.0, 32.0)
        out = 0
        for n, (s, cuts) in enumerate(mine):
            for m in range(batches):
                at = n * CORES * part + m * rows_own
                t = jnp.where(live[s][m], y[at : at + rows_own], 0.0)
                o, mm = out + m // (batches // cuts), m % (batches // cuts)
                outs[o][mm, :, c * blk : (c + 1) * blk] = t.astype(jnp.bfloat16)
            out += cuts


def body(features, weights, sources, bias, batch_rows):
    sections = lax.axis_size("section")
    cols = lax.axis_size("col")
    zs = cols // CORES
    w = weights[0]
    blocks_own, knz, blk, _ = w.shape
    batches, rows_own, _ = features.shape
    need = cols * CAP
    half = batches * rows_own * sections // CORES
    part = half // sections
    bf, i32, f32 = jnp.bfloat16, jnp.int32, jnp.float32
    S = jax.ShapeDtypeStruct
    section = lax.axis_index("section")

    def room(mib):
        return pltpu.CompilerParams(vmem_limit_bytes=mib << 20)

    ask, slot = pl.pallas_call(
        functools.partial(pool_kernel, cols, blocks_own),
        out_shape=(S((sections * cols, 1, CORES * CAP), i32), S((knz, blocks_own), i32)),
        in_specs=[VM],
        out_specs=(VM, VM),
        compiler_params=room(46),
        name="pools",
    )(sources[0].T)
    got = lax.all_to_all(ask, BOTH, 0, 0, tiled=True)

    total = sections * cols
    sibling = [(i, i ^ 1) for i in range(total)]
    w3 = w.reshape(blocks_own, knz * blk, blk)
    b3 = bias[0].reshape(blocks_own, 1, blk)
    w_then, _ = lax.optimization_barrier((w3, got))
    sw3 = lax.ppermute(w_then, BOTH, sibling)
    sb3 = lax.ppermute(b3, BOTH, sibling)
    sib_slot = lax.ppermute(slot, BOTH, sibling)

    sends = pl.pallas_call(
        functools.partial(feature_kernel, cols),
        out_shape=S((sections * cols, CORES * CAP, batches // CORES, rows_own, blk), bf),
        in_specs=[SM, VM],
        out_specs=HB,
        scratch_shapes=[
            pltpu.VMEM((cols, CORES * CAP, batches // CORES, rows_own, blk), bf),
            pltpu.SemaphoreType.DMA,
        ],
        compiler_params=room(56),
        name="gather_features",
    )(got, features)
    recv = lax.all_to_all(sends.reshape(sections * cols, CORES * CAP, part, blk), BOTH, 0, 0, tiled=True)

    layer_args = pl.pallas_call(
        functools.partial(prepare_kernel, sections, cols),
        out_shape=(S((need, knz * blk, blk), bf), S((CORES * need, 1, blk), f32), S((knz + 1, CORES * need), i32)),
        in_specs=[SM, SM, SM, HB, VM, VM],
        out_specs=(VM, VM, SM),
        scratch_shapes=[pltpu.SemaphoreType.DMA((need,))],
        compiler_params=room(46),
        name="prepare",
    )(got, slot, sib_slot, w3, b3, sb3)
    layer_specs = [VM, VM, SM]
    piece = S((CORES * CORES * CAP, half, blk), bf)
    scratch = [pltpu.VMEM((CORES * need, half, blk), bf)]
    params = room(24)

    def shift(xs, layer):
        def pairs(dz):
            return [(layer * cols + e, (layer + 1) * cols + (e + CORES * dz) % cols) for e in range(cols)]

        order = sorted(range(zs), key=lambda dz: -min(dz, zs - dz))
        ys = {dz: lax.ppermute(xs[dz], BOTH, pairs(dz)) for dz in order}
        if 0 < layer < sections - 2:
            lead, *later = order
            ys[lead] = pl.pallas_call(
                take_kernel, out_shape=piece, in_specs=[VM], out_specs=VM, compiler_params=params, name="take"
            )(ys[lead])
            for dz, y in zip(order, lax.optimization_barrier(tuple(ys[dz] for dz in order))):
                ys[dz] = y
        return [ys[dz] for dz in range(zs)]

    *xs, ws = pl.pallas_call(
        functools.partial(first_kernel, sections, zs, blk),
        out_shape=(piece,) * zs + (S((need, knz * blk, blk), bf),),
        in_specs=[VM] + layer_specs + [HB],
        out_specs=(VM,) * (zs + 1),
        scratch_shapes=scratch + [pltpu.SemaphoreType.DMA((need,))],
        compiler_params=room(44),
        name="first_layer",
    )(recv, *layer_args, sw3)
    xs = shift(xs, 0)
    for layer in range(1, sections - 1):
        xs = pl.pallas_call(
            functools.partial(middle_kernel, zs, blk, layer),
            out_shape=(piece,) * zs,
            in_specs=[VM] * zs + layer_specs + [VM],
            out_specs=(VM,) * zs,
            scratch_shapes=scratch,
            compiler_params=params,
            name="middle_layer",
        )(*xs, *layer_args, ws)
        ready = xs[0]
        xs = shift(xs, layer)

    w_late, _ = lax.optimization_barrier((w3, ready))
    wv = pl.pallas_call(
        functools.partial(resident_kernel, sections),
        out_shape=S(w3.shape, bf),
        in_specs=[HB],
        out_specs=VM,
        scratch_shapes=[pltpu.SemaphoreType.DMA],
        cost_estimate=pl.CostEstimate(flops=0, bytes_accessed=w3.size * 4, transcendentals=0),
        compiler_params=room(40),
        name="resident_weights",
    )(w_late)
    *xs, wv = lax.optimization_barrier((*xs, wv))

    core = lax.rem(lax.axis_index("col"), CORES)
    per = CORES * CAP
    give = jnp.stack([lax.dynamic_slice_in_dim(x, (1 - core) * per, per, 0) for x in xs])
    sib = lax.ppermute(give, BOTH, sibling)

    relays = {0: 1} if sections == 4 and batches % 2 == 0 else {}
    last = sections - 1
    per_section = half * CORES // sections

    def last_call(mine, first, operands, name):
        shapes = [
            S((batches // cuts, rows_own, blocks_own * blk), bf) for _, cuts in mine for _ in range(cuts)
        ]
        if first:
            shapes.append(S((sections, need, per_section, blk), bf))
        return pl.pallas_call(
            functools.partial(last_kernel, zs, sections, rows_own, mine, first),
            out_shape=tuple(shapes),
            in_specs=[VM] * (len(operands) - 4) + [SM, SM, VM, VM],
            out_specs=(VM,) * len(shapes),
            compiler_params=params,
            name=name,
        )(*operands)

    mine = [(s, 2 if s in relays else 1) for s in range(sections)]
    *outs, pool = last_call(mine[:1], True, (*xs, sib, slot, batch_rows, wv, bias), "last_layer")
    outs += last_call(mine[1:], False, (pool, slot, batch_rows, wv, bias), "last_layer_rest")

    def send(x, a, b):
        return lax.ppermute(x, BOTH, [(a * cols + e, b * cols + e) for e in range(cols)])

    there = {}
    for s in range(sections - 1):
        if s in relays:
            via = relays[s]
            hop = send(outs.pop(0), last, via)
            direct = send(outs.pop(0), last, s)
            there[s] = (hop, via, direct)
        else:
            there[s] = send(outs.pop(0), last, s)
    result = outs[-1]
    for s in range(sections - 1):
        if s in relays:
            hop, via, direct = there[s]
            hop, direct = lax.optimization_barrier((hop, direct))
            there[s] = jnp.concatenate([send(hop, via, s), direct], axis=0)
        result = jnp.where(section == s, there[s], result)
    return result


def solution(mesh):
    in_specs = (
        P(None, "section", "col"),
        P("section", "col", None, None, None),
        P("section", "col", None),
        P("section", "col"),
        P(),
    )
    out_specs = P(None, "section", "col")
    return jax.shard_map(body, mesh=mesh, in_specs=in_specs, out_specs=out_specs, check_vma=False)
```

```python
import functools

import jax
import jax.numpy as jnp
from jax import lax
from jax.experimental import pallas as pl
from jax.experimental.pallas import tpu as pltpu
from jax.sharding import PartitionSpec as P

CAP = 2
CORES = 2
BOTH = ("section", "col")
VM = pl.BlockSpec(memory_space=pltpu.VMEM)
SM = pl.BlockSpec(memory_space=pltpu.SMEM)
HB = pl.BlockSpec(memory_space=pl.ANY)
BIG = 1 << 30


def pool_kernel(cols, blocks_own, src_ref, ask_ref, slot_ref):
    src = src_ref[...]
    owner = src // blocks_own
    slot = jnp.zeros_like(src)
    lows, highs = [], []
    for e in range(cols):
        mine = owner == e
        low = jnp.min(jnp.where(mine, src, BIG), axis=(0, 1), keepdims=True)
        high = jnp.max(jnp.where(mine, src, -1), axis=(0, 1), keepdims=True)
        slot = jnp.where(mine, CAP * e + (src > low).astype(jnp.int32), slot)
        lows.append(low - e * blocks_own)
        highs.append(high - e * blocks_own)
    slot_ref[...] = slot
    for e in range(cols):
        o = e ^ 1
        both = jnp.concatenate([lows[e], highs[e], lows[o], highs[o]], axis=1)
        for s in range(ask_ref.shape[0] // cols):
            ask_ref[s * cols + e] = both


def prepare_kernel(sections, cols, got_ref, slot_ref, sib_slot_ref, w_ref, b_ref, sb_ref, wo_ref, bo_ref, info_ref, sem):
    nxt = jnp.minimum(lax.axis_index("section") + 1, sections - 1)
    need = cols * CAP
    copies = []
    for i in range(need):
        c = got_ref[nxt * cols + i // CAP, 0, i % CAP]
        copies.append(pltpu.make_async_copy(w_ref.at[c], wo_ref.at[i], sem.at[i]))
        copies[-1].start()
    for r, (slots, src) in enumerate(((slot_ref, b_ref), (sib_slot_ref, sb_ref))):
        for i in range(need):
            c = got_ref[nxt * cols + i // CAP, 0, r * CAP + i % CAP]
            bo_ref[r * need + i] = src[c]
            for k in range(slots.shape[0]):
                info_ref[k, r * need + i] = slots[k, c]
            info_ref[slots.shape[0], r * need + i] = c
    for copy in copies:
        copy.wait()


def resident_kernel(sections, w_ref, wv_ref, sem):
    @pl.when(lax.axis_index("section") == sections - 1)
    def _():
        copy = pltpu.make_async_copy(w_ref, wv_ref, sem)
        copy.start()
        copy.wait()


def feature_kernel(cols, got_ref, feat_ref, out_ref, near, sem):
    blk = near.shape[4]
    half = near.shape[2]
    for z in range(cols // CORES):
        for cd in range(CORES):
            for j in range(CAP):
                b = got_ref[z * CORES + cd, 0, j]
                at = pl.ds(pl.multiple_of(b * blk, blk), blk)
                for cp in range(CORES):
                    near[z * CORES + cp, cd * CAP + j] = feat_ref[cp * half : (cp + 1) * half, :, at]
    copy = pltpu.make_async_copy(near, out_ref.at[pl.ds(0, cols)], sem)
    copy.start()
    copy.wait()


def way(step, core, zs):
    return lax.rem(step + core * (zs // 2), zs) if not isinstance(core, int) else (step + core * (zs // 2)) % zs


def run_layer(zs, blk, core, rel, pool, w, b, info, outs):
    z = lax.axis_index("col") // CORES
    knz = info.shape[0] - 1
    need = zs * CORES * CAP
    cc = lax.rem(core + rel, CORES)
    for dz in range(zs):
        zd = lax.rem(z + way(dz, core, zs), zs)
        for cd in range(CORES):
            for j in range(CAP):
                i = (zd * CORES + cd) * CAP + j
                at = rel * need + i
                x = jnp.concatenate([pool[cc * need + info[k, at]] for k in range(knz)], axis=1)
                y = jnp.dot(x, w[i], preferred_element_type=jnp.float32) + b[at]
                outs[dz][cd * (CORES * CAP) + cc * CAP + j] = jnp.clip(y, 0.0, 32.0).astype(jnp.bfloat16)


def first_kernel(sections, zs, blk, recv_ref, w, b, info, sw_ref, *rest):
    outs, ws, pool, sem = rest[:zs], rest[zs], rest[zs + 1], rest[zs + 2]
    part = recv_ref.shape[2]
    cols = zs * CORES
    need = cols * CAP
    core = lax.rem(lax.axis_index("col"), CORES)
    here = lax.axis_index("section") == 0
    copies = []
    for i in range(need):
        copies.append(pltpu.make_async_copy(sw_ref.at[info[info.shape[0] - 1, need + i]], ws.at[i], sem.at[i]))
        copies[-1].start()

    @pl.when(here)
    def _():
        for s in range(sections):
            for e in range(cols):
                for cd in range(CORES):
                    for j in range(CAP):
                        pool[cd * need + e * CAP + j, s * part : (s + 1) * part] = recv_ref[s * cols + e, cd * CAP + j]
        run_layer(zs, blk, core, 0, pool, w, b, info, outs)

    for copy in copies:
        copy.wait()

    @pl.when(here)
    def _():
        run_layer(zs, blk, core, 1, pool, ws, b, info, outs)


def take_kernel(x_ref, o_ref):
    o_ref[...] = x_ref[...]


def middle_kernel(zs, blk, layer, *refs):
    ins, (w, b, info, ws), outs, pool = refs[:zs], refs[zs : zs + 4], refs[zs + 4 : -1], refs[-1]
    cols = zs * CORES
    z = lax.axis_index("col") // CORES
    core = lax.rem(lax.axis_index("col"), CORES)
    per = CORES * CAP

    @pl.when(lax.axis_index("section") == layer)
    def _():
        for dz in range(zs):
            ze = lax.rem(z - way(dz, core, zs) + zs, zs)
            for cd in range(CORES):
                for q in range(per):
                    pool[cd * cols * CAP + ze * per + q] = ins[dz][cd * per + q]
        run_layer(zs, blk, core, 0, pool, w, b, info, outs)
        run_layer(zs, blk, core, 1, pool, ws, b, info, outs)


def last_kernel(zs, sections, rows_own, mine, first, *refs):
    @pl.when(lax.axis_index("section") == sections - 1)
    def _():
        last_layer(zs, sections, rows_own, mine, first, *refs)


def last_layer(zs, sections, rows_own, mine, first, *refs):
    if first:
        ins, sib, refs = refs[:zs], refs[zs], refs[zs + 1 :]
        slot, rows_ref, w_ref, b_ref, *outs, pool = refs
    else:
        pool, slot, rows_ref, w_ref, b_ref, *outs = refs
    col = lax.axis_index("col")
    z, core = col // CORES, lax.rem(col, CORES)
    per = CORES * CAP
    blk = pool.shape[3]
    batches = rows_ref.shape[0]
    part = pool.shape[2] // CORES
    if first:
        for dz in range(zs):
            ze = lax.rem(z - way(dz, core, zs) + zs, zs)
            zo = lax.rem(z - way(dz, 1 - core, zs) + zs, zs)
            for q in range(per):
                for s in range(sections):
                    rows = slice(s * part, (s + 1) * part)
                    own, other = ins[dz][core * per + q, rows], sib[dz, q, rows]
                    if part % 16 == 0:
                        pool[s, ze * per + q, pl.ds(pl.multiple_of(core * part, part), part), :] = own
                        pool[s, zo * per + q, pl.ds(pl.multiple_of((1 - core) * part, part), part), :] = other
                    else:
                        for h in range(CORES):
                            at = jnp.where(core == h, ze, zo) * per + q
                            pool[s, at, h * part : (h + 1) * part] = jnp.where(core == h, own, other)

    columns, knz = w_ref.shape[0], slot.shape[0]
    ids = lax.broadcasted_iota(jnp.int32, (rows_own, 1), 0)
    live = {s: [(s * rows_own + ids) < rows_ref[m] for m in range(batches)] for s, _ in mine}
    for c in range(columns):
        x = jnp.concatenate(
            [
                jnp.concatenate([pool[s, slot[k, c]] for k in range(knz)], axis=1)
                for s, _ in mine
            ],
            axis=0,
        )
        y = jnp.dot(x, w_ref[c], preferred_element_type=jnp.float32) + b_ref[:, c * blk : (c + 1) * blk]
        y = jnp.clip(y, 0.0, 32.0)
        out = 0
        for n, (s, cuts) in enumerate(mine):
            for m in range(batches):
                at = n * CORES * part + m * rows_own
                t = jnp.where(live[s][m], y[at : at + rows_own], 0.0)
                o, mm = out + m // (batches // cuts), m % (batches // cuts)
                outs[o][mm, :, c * blk : (c + 1) * blk] = t.astype(jnp.bfloat16)
            out += cuts


def body(features, weights, sources, bias, batch_rows):
    sections = lax.axis_size("section")
    cols = lax.axis_size("col")
    zs = cols // CORES
    w = weights[0]
    blocks_own, knz, blk, _ = w.shape
    batches, rows_own, _ = features.shape
    need = cols * CAP
    half = batches * rows_own * sections // CORES
    part = half // sections
    bf, i32, f32 = jnp.bfloat16, jnp.int32, jnp.float32
    S = jax.ShapeDtypeStruct
    section = lax.axis_index("section")

    def room(mib):
        return pltpu.CompilerParams(vmem_limit_bytes=mib << 20)

    ask, slot = pl.pallas_call(
        functools.partial(pool_kernel, cols, blocks_own),
        out_shape=(S((sections * cols, 1, CORES * CAP), i32), S((knz, blocks_own), i32)),
        in_specs=[VM],
        out_specs=(VM, VM),
        compiler_params=room(46),
        name="pools",
    )(sources[0].T)
    got = lax.all_to_all(ask, BOTH, 0, 0, tiled=True)

    total = sections * cols
    sibling = [(i, i ^ 1) for i in range(total)]
    w3 = w.reshape(blocks_own, knz * blk, blk)
    b3 = bias[0].reshape(blocks_own, 1, blk)
    w_then, _ = lax.optimization_barrier((w3, got))
    sw3 = lax.ppermute(w_then, BOTH, sibling)
    sb3 = lax.ppermute(b3, BOTH, sibling)
    sib_slot = lax.ppermute(slot, BOTH, sibling)

    sends = pl.pallas_call(
        functools.partial(feature_kernel, cols),
        out_shape=S((sections * cols, CORES * CAP, batches // CORES, rows_own, blk), bf),
        in_specs=[SM, VM],
        out_specs=HB,
        scratch_shapes=[
            pltpu.VMEM((cols, CORES * CAP, batches // CORES, rows_own, blk), bf),
            pltpu.SemaphoreType.DMA,
        ],
        compiler_params=room(56),
        name="gather_features",
    )(got, features)
    recv = lax.all_to_all(sends.reshape(sections * cols, CORES * CAP, part, blk), BOTH, 0, 0, tiled=True)

    layer_args = pl.pallas_call(
        functools.partial(prepare_kernel, sections, cols),
        out_shape=(S((need, knz * blk, blk), bf), S((CORES * need, 1, blk), f32), S((knz + 1, CORES * need), i32)),
        in_specs=[SM, SM, SM, HB, VM, VM],
        out_specs=(VM, VM, SM),
        scratch_shapes=[pltpu.SemaphoreType.DMA((need,))],
        compiler_params=room(46),
        name="prepare",
    )(got, slot, sib_slot, w3, b3, sb3)
    layer_specs = [VM, VM, SM]
    piece = S((CORES * CORES * CAP, half, blk), bf)
    scratch = [pltpu.VMEM((CORES * need, half, blk), bf)]
    params = room(24)

    def shift(xs, layer):
        def pairs(dz):
            return [(layer * cols + e, (layer + 1) * cols + (e + CORES * way(dz, e % CORES, zs)) % cols) for e in range(cols)]

        order = sorted(range(zs), key=lambda dz: -min(dz, zs - dz))
        ys = {dz: lax.ppermute(xs[dz], BOTH, pairs(dz)) for dz in order}
        if 0 < layer < sections - 2:
            lead, *later = order
            ys[lead] = pl.pallas_call(
                take_kernel, out_shape=piece, in_specs=[VM], out_specs=VM, compiler_params=params, name="take"
            )(ys[lead])
            for dz, y in zip(order, lax.optimization_barrier(tuple(ys[dz] for dz in order))):
                ys[dz] = y
        return [ys[dz] for dz in range(zs)]

    *xs, ws = pl.pallas_call(
        functools.partial(first_kernel, sections, zs, blk),
        out_shape=(piece,) * zs + (S((need, knz * blk, blk), bf),),
        in_specs=[VM] + layer_specs + [HB],
        out_specs=(VM,) * (zs + 1),
        scratch_shapes=scratch + [pltpu.SemaphoreType.DMA((need,))],
        compiler_params=room(44),
        name="first_layer",
    )(recv, *layer_args, sw3)
    xs = shift(xs, 0)
    for layer in range(1, sections - 1):
        xs = pl.pallas_call(
            functools.partial(middle_kernel, zs, blk, layer),
            out_shape=(piece,) * zs,
            in_specs=[VM] * zs + layer_specs + [VM],
            out_specs=(VM,) * zs,
            scratch_shapes=scratch,
            compiler_params=params,
            name="middle_layer",
        )(*xs, *layer_args, ws)
        ready = xs[0]
        xs = shift(xs, layer)

    w_late, _ = lax.optimization_barrier((w3, ready))
    wv = pl.pallas_call(
        functools.partial(resident_kernel, sections),
        out_shape=S(w3.shape, bf),
        in_specs=[HB],
        out_specs=VM,
        scratch_shapes=[pltpu.SemaphoreType.DMA],
        cost_estimate=pl.CostEstimate(flops=0, bytes_accessed=w3.size * 4, transcendentals=0),
        compiler_params=room(40),
        name="resident_weights",
    )(w_late)
    *xs, wv = lax.optimization_barrier((*xs, wv))

    core = lax.rem(lax.axis_index("col"), CORES)
    per = CORES * CAP
    give = jnp.stack([lax.dynamic_slice_in_dim(x, (1 - core) * per, per, 0) for x in xs])
    sib = lax.ppermute(give, BOTH, sibling)

    relays = {0: 1} if sections == 4 and batches % 2 == 0 else {}
    last = sections - 1
    per_section = half * CORES // sections

    def last_call(mine, first, operands, name):
        shapes = [
            S((batches // cuts, rows_own, blocks_own * blk), bf) for _, cuts in mine for _ in range(cuts)
        ]
        if first:
            shapes.append(S((sections, need, per_section, blk), bf))
        return pl.pallas_call(
            functools.partial(last_kernel, zs, sections, rows_own, mine, first),
            out_shape=tuple(shapes),
            in_specs=[VM] * (len(operands) - 4) + [SM, SM, VM, VM],
            out_specs=(VM,) * len(shapes),
            compiler_params=params,
            name=name,
        )(*operands)

    mine = [(s, 2 if s in relays else 1) for s in range(sections)]
    *outs, pool = last_call(mine[:1], True, (*xs, sib, slot, batch_rows, wv, bias), "last_layer")
    outs += last_call(mine[1:], False, (pool, slot, batch_rows, wv, bias), "last_layer_rest")

    def send(x, a, b):
        return lax.ppermute(x, BOTH, [(a * cols + e, b * cols + e) for e in range(cols)])

    there = {}
    for s in range(sections - 1):
        if s in relays:
            via = relays[s]
            hop = send(outs.pop(0), last, via)
            direct = send(outs.pop(0), last, s)
            there[s] = (hop, via, direct)
        else:
            there[s] = send(outs.pop(0), last, s)
    result = outs[-1]
    for s in range(sections - 1):
        if s in relays:
            hop, via, direct = there[s]
            hop, direct = lax.optimization_barrier((hop, direct))
            there[s] = jnp.concatenate([send(hop, via, s), direct], axis=0)
        result = jnp.where(section == s, there[s], result)
    return result


def solution(mesh):
    in_specs = (
        P(None, "section", "col"),
        P("section", "col", None, None, None),
        P("section", "col", None),
        P("section", "col"),
        P(),
    )
    out_specs = P(None, "section", "col")
    return jax.shard_map(body, mesh=mesh, in_specs=in_specs, out_specs=out_specs, check_vma=False)
```

```python
import functools

import jax
import jax.numpy as jnp
from jax import lax
from jax.experimental import pallas as pl
from jax.experimental.pallas import tpu as pltpu
from jax.sharding import PartitionSpec as P

CAP = 2
CORES = 2
BOTH = ("section", "col")
VM = pl.BlockSpec(memory_space=pltpu.VMEM)
SM = pl.BlockSpec(memory_space=pltpu.SMEM)
HB = pl.BlockSpec(memory_space=pl.ANY)
BIG = 1 << 30


def pool_kernel(cols, blocks_own, src_ref, ask_ref, slot_ref):
    src = src_ref[...]
    owner = src // blocks_own
    slot = jnp.zeros_like(src)
    lows, highs = [], []
    for e in range(cols):
        mine = owner == e
        low = jnp.min(jnp.where(mine, src, BIG), axis=(0, 1), keepdims=True)
        high = jnp.max(jnp.where(mine, src, -1), axis=(0, 1), keepdims=True)
        slot = jnp.where(mine, CAP * e + (src > low).astype(jnp.int32), slot)
        lows.append(low - e * blocks_own)
        highs.append(high - e * blocks_own)
    slot_ref[...] = slot
    for e in range(cols):
        o = e ^ 1
        both = jnp.concatenate([lows[e], highs[e], lows[o], highs[o]], axis=1)
        for s in range(ask_ref.shape[0] // cols):
            ask_ref[s * cols + e] = both


def prepare_kernel(sections, cols, got_ref, slot_ref, sib_slot_ref, w_ref, b_ref, sb_ref, wo_ref, bo_ref, info_ref, sem):
    nxt = jnp.minimum(lax.axis_index("section") + 1, sections - 1)
    need = cols * CAP
    copies = []
    for i in range(need):
        c = got_ref[nxt * cols + i // CAP, 0, i % CAP]
        copies.append(pltpu.make_async_copy(w_ref.at[c], wo_ref.at[i], sem.at[i]))
        copies[-1].start()
    for r, (slots, src) in enumerate(((slot_ref, b_ref), (sib_slot_ref, sb_ref))):
        for i in range(need):
            c = got_ref[nxt * cols + i // CAP, 0, r * CAP + i % CAP]
            bo_ref[r * need + i] = src[c]
            for k in range(slots.shape[0]):
                info_ref[k, r * need + i] = slots[k, c]
            info_ref[slots.shape[0], r * need + i] = c
    for copy in copies:
        copy.wait()


def resident_kernel(sections, w_ref, wv_ref, sem):
    @pl.when(lax.axis_index("section") == sections - 1)
    def _():
        copy = pltpu.make_async_copy(w_ref, wv_ref, sem)
        copy.start()
        copy.wait()


def feature_kernel(cols, got_ref, feat_ref, out_ref):
    batches, rows, _ = feat_ref.shape
    blk = out_ref.shape[3]
    half = batches // CORES
    for z in range(cols // CORES):
        for cd in range(CORES):
            for j in range(CAP):
                b = got_ref[z * CORES + cd, 0, j]
                x = feat_ref[:, :, pl.ds(pl.multiple_of(b * blk, blk), blk)].astype(jnp.float32)
                x = x.reshape(batches * rows, blk).astype(jnp.bfloat16)
                for cp in range(CORES):
                    out_ref[z * CORES + cp, cd * CAP + j] = x[cp * half * rows : (cp + 1) * half * rows]


def way(step, core, zs):
    return (step + core * (zs // 2)) % zs if isinstance(core, int) else lax.rem(step + core * (zs // 2), zs)


def run_layer(zs, blk, core, rel, pool, w, b, info, outs):
    z = lax.axis_index("col") // CORES
    knz = info.shape[0] - 1
    need = zs * CORES * CAP
    cc = lax.rem(core + rel, CORES)
    for dz in range(zs):
        zd = lax.rem(z + way(dz, core, zs), zs)
        for cd in range(CORES):
            for j in range(CAP):
                i = (zd * CORES + cd) * CAP + j
                at = rel * need + i
                x = jnp.concatenate([pool[cc * need + info[k, at]] for k in range(knz)], axis=1)
                y = jnp.dot(x, w[i], preferred_element_type=jnp.float32) + b[at]
                outs[dz][cd * (CORES * CAP) + cc * CAP + j] = jnp.clip(y, 0.0, 32.0).astype(jnp.bfloat16)


def first_kernel(sections, zs, blk, recv_ref, w, b, info, sw_ref, *rest):
    outs, ws, pool, sem = rest[:zs], rest[zs], rest[zs + 1], rest[zs + 2]
    part = recv_ref.shape[2]
    cols = zs * CORES
    need = cols * CAP
    core = lax.rem(lax.axis_index("col"), CORES)
    here = lax.axis_index("section") == 0
    copies = []
    for i in range(need):
        copies.append(pltpu.make_async_copy(sw_ref.at[info[info.shape[0] - 1, need + i]], ws.at[i], sem.at[i]))
        copies[-1].start()

    @pl.when(here)
    def _():
        for s in range(sections):
            for e in range(cols):
                for cd in range(CORES):
                    for j in range(CAP):
                        pool[cd * need + e * CAP + j, s * part : (s + 1) * part] = recv_ref[s * cols + e, cd * CAP + j]
        run_layer(zs, blk, core, 0, pool, w, b, info, outs)

    for copy in copies:
        copy.wait()

    @pl.when(here)
    def _():
        run_layer(zs, blk, core, 1, pool, ws, b, info, outs)


def take_kernel(x_ref, o_ref):
    o_ref[...] = x_ref[...]


def middle_kernel(zs, blk, layer, *refs):
    ins, (w, b, info, ws), outs, pool = refs[:zs], refs[zs : zs + 4], refs[zs + 4 : -1], refs[-1]
    cols = zs * CORES
    z = lax.axis_index("col") // CORES
    core = lax.rem(lax.axis_index("col"), CORES)
    per = CORES * CAP

    @pl.when(lax.axis_index("section") == layer)
    def _():
        for dz in range(zs):
            ze = lax.rem(z - way(dz, core, zs) + zs, zs)
            for cd in range(CORES):
                for q in range(per):
                    pool[cd * cols * CAP + ze * per + q] = ins[dz][cd * per + q]
        run_layer(zs, blk, core, 0, pool, w, b, info, outs)
        run_layer(zs, blk, core, 1, pool, ws, b, info, outs)


def last_kernel(zs, sections, rows_own, mine, first, *refs):
    @pl.when(lax.axis_index("section") == sections - 1)
    def _():
        last_layer(zs, sections, rows_own, mine, first, *refs)


def last_layer(zs, sections, rows_own, mine, first, *refs):
    if first:
        ins, sib, refs = refs[:zs], refs[zs], refs[zs + 1 :]
        slot, rows_ref, w_ref, b_ref, *outs, pool = refs
    else:
        pool, slot, rows_ref, w_ref, b_ref, *outs = refs
    col = lax.axis_index("col")
    z, core = col // CORES, lax.rem(col, CORES)
    per = CORES * CAP
    blk = pool.shape[3]
    batches = rows_ref.shape[0]
    part = pool.shape[2] // CORES
    if first:
        for dz in range(zs):
            ze = lax.rem(z - way(dz, core, zs) + zs, zs)
            zo = lax.rem(z - way(dz, 1 - core, zs) + zs, zs)
            for q in range(per):
                for s in range(sections):
                    rows = slice(s * part, (s + 1) * part)
                    own, other = ins[dz][core * per + q, rows], sib[dz, q, rows]
                    if part % 16 == 0:
                        pool[s, ze * per + q, pl.ds(pl.multiple_of(core * part, part), part), :] = own
                        pool[s, zo * per + q, pl.ds(pl.multiple_of((1 - core) * part, part), part), :] = other
                    else:
                        for h in range(CORES):
                            at = jnp.where(core == h, ze, zo) * per + q
                            pool[s, at, h * part : (h + 1) * part] = jnp.where(core == h, own, other)

    columns, knz = w_ref.shape[0], slot.shape[0]
    ids = lax.broadcasted_iota(jnp.int32, (rows_own, 1), 0)
    live = {s: [(s * rows_own + ids) < rows_ref[m] for m in range(batches)] for s, _ in mine}
    for c in range(columns):
        x = jnp.concatenate(
            [
                jnp.concatenate([pool[s, slot[k, c]] for k in range(knz)], axis=1)
                for s, _ in mine
            ],
            axis=0,
        )
        y = jnp.dot(x, w_ref[c], preferred_element_type=jnp.float32) + b_ref[:, c * blk : (c + 1) * blk]
        y = jnp.clip(y, 0.0, 32.0)
        out = 0
        for n, (s, cuts) in enumerate(mine):
            for m in range(batches):
                at = n * CORES * part + m * rows_own
                t = jnp.where(live[s][m], y[at : at + rows_own], 0.0)
                o, mm = out + m // (batches // cuts), m % (batches // cuts)
                outs[o][mm, :, c * blk : (c + 1) * blk] = t.astype(jnp.bfloat16)
            out += cuts


def body(features, weights, sources, bias, batch_rows):
    sections = lax.axis_size("section")
    cols = lax.axis_size("col")
    zs = cols // CORES
    w = weights[0]
    blocks_own, knz, blk, _ = w.shape
    batches, rows_own, _ = features.shape
    need = cols * CAP
    half = batches * rows_own * sections // CORES
    part = half // sections
    bf, i32, f32 = jnp.bfloat16, jnp.int32, jnp.float32
    S = jax.ShapeDtypeStruct
    section = lax.axis_index("section")

    def room(mib):
        return pltpu.CompilerParams(vmem_limit_bytes=mib << 20)

    ask, slot = pl.pallas_call(
        functools.partial(pool_kernel, cols, blocks_own),
        out_shape=(S((sections * cols, 1, CORES * CAP), i32), S((knz, blocks_own), i32)),
        in_specs=[VM],
        out_specs=(VM, VM),
        compiler_params=room(46),
        name="pools",
    )(sources[0].T)
    got = lax.all_to_all(ask, BOTH, 0, 0, tiled=True)

    total = sections * cols
    sibling = [(i, i ^ 1) for i in range(total)]
    w3 = w.reshape(blocks_own, knz * blk, blk)
    b3 = bias[0].reshape(blocks_own, 1, blk)
    w_then, _ = lax.optimization_barrier((w3, got))
    sw3 = lax.ppermute(w_then, BOTH, sibling)
    sb3 = lax.ppermute(b3, BOTH, sibling)
    sib_slot = lax.ppermute(slot, BOTH, sibling)

    sends = pl.pallas_call(
        functools.partial(feature_kernel, cols),
        out_shape=S((sections * cols, CORES * CAP, part, blk), bf),
        in_specs=[SM, VM],
        out_specs=VM,
        compiler_params=room(56),
        name="gather_features",
    )(got, features)
    recv = lax.all_to_all(sends, BOTH, 0, 0, tiled=True)

    layer_args = pl.pallas_call(
        functools.partial(prepare_kernel, sections, cols),
        out_shape=(S((need, knz * blk, blk), bf), S((CORES * need, 1, blk), f32), S((knz + 1, CORES * need), i32)),
        in_specs=[SM, SM, SM, HB, VM, VM],
        out_specs=(VM, VM, SM),
        scratch_shapes=[pltpu.SemaphoreType.DMA((need,))],
        compiler_params=room(46),
        name="prepare",
    )(got, slot, sib_slot, w3, b3, sb3)
    layer_specs = [VM, VM, SM]
    piece = S((CORES * CORES * CAP, half, blk), bf)
    scratch = [pltpu.VMEM((CORES * need, half, blk), bf)]
    params = room(24)

    def shift(xs, layer):
        def pairs(dz):
            return [(layer * cols + e, (layer + 1) * cols + (e + CORES * way(dz, e % CORES, zs)) % cols) for e in range(cols)]

        order = sorted(range(zs), key=lambda dz: -min(dz, zs - dz))
        ys = {dz: lax.ppermute(xs[dz], BOTH, pairs(dz)) for dz in order}
        if 0 < layer < sections - 2:
            lead, *later = order
            ys[lead] = pl.pallas_call(
                take_kernel, out_shape=piece, in_specs=[VM], out_specs=VM, compiler_params=params, name="take"
            )(ys[lead])
            for dz, y in zip(order, lax.optimization_barrier(tuple(ys[dz] for dz in order))):
                ys[dz] = y
        return [ys[dz] for dz in range(zs)]

    *xs, ws = pl.pallas_call(
        functools.partial(first_kernel, sections, zs, blk),
        out_shape=(piece,) * zs + (S((need, knz * blk, blk), bf),),
        in_specs=[VM] + layer_specs + [HB],
        out_specs=(VM,) * (zs + 1),
        scratch_shapes=scratch + [pltpu.SemaphoreType.DMA((need,))],
        compiler_params=room(44),
        name="first_layer",
    )(recv, *layer_args, sw3)
    xs = shift(xs, 0)
    for layer in range(1, sections - 1):
        xs = pl.pallas_call(
            functools.partial(middle_kernel, zs, blk, layer),
            out_shape=(piece,) * zs,
            in_specs=[VM] * zs + layer_specs + [VM],
            out_specs=(VM,) * zs,
            scratch_shapes=scratch,
            compiler_params=params,
            name="middle_layer",
        )(*xs, *layer_args, ws)
        ready = xs[0]
        xs = shift(xs, layer)

    w_late, _ = lax.optimization_barrier((w3, ready))
    wv = pl.pallas_call(
        functools.partial(resident_kernel, sections),
        out_shape=S(w3.shape, bf),
        in_specs=[HB],
        out_specs=VM,
        scratch_shapes=[pltpu.SemaphoreType.DMA],
        cost_estimate=pl.CostEstimate(flops=0, bytes_accessed=w3.size * 4, transcendentals=0),
        compiler_params=room(40),
        name="resident_weights",
    )(w_late)
    *xs, wv = lax.optimization_barrier((*xs, wv))

    core = lax.rem(lax.axis_index("col"), CORES)
    per = CORES * CAP
    give = jnp.stack([lax.dynamic_slice_in_dim(x, (1 - core) * per, per, 0) for x in xs])
    sib = lax.ppermute(give, BOTH, sibling)

    relays = {0: 1} if sections == 4 and batches % 2 == 0 else {}
    last = sections - 1
    per_section = half * CORES // sections

    def last_call(mine, first, operands, name):
        shapes = [
            S((batches // cuts, rows_own, blocks_own * blk), bf) for _, cuts in mine for _ in range(cuts)
        ]
        if first:
            shapes.append(S((sections, need, per_section, blk), bf))
        return pl.pallas_call(
            functools.partial(last_kernel, zs, sections, rows_own, mine, first),
            out_shape=tuple(shapes),
            in_specs=[VM] * (len(operands) - 4) + [SM, SM, VM, VM],
            out_specs=(VM,) * len(shapes),
            compiler_params=params,
            name=name,
        )(*operands)

    mine = [(s, 2 if s in relays else 1) for s in range(sections)]
    *outs, pool = last_call(mine[:1], True, (*xs, sib, slot, batch_rows, wv, bias), "last_layer")
    outs += last_call(mine[1:], False, (pool, slot, batch_rows, wv, bias), "last_layer_rest")

    def send(x, a, b):
        return lax.ppermute(x, BOTH, [(a * cols + e, b * cols + e) for e in range(cols)])

    there = {}
    for s in range(sections - 1):
        if s in relays:
            via = relays[s]
            hop = send(outs.pop(0), last, via)
            direct = send(outs.pop(0), last, s)
            there[s] = (hop, via, direct)
        else:
            there[s] = send(outs.pop(0), last, s)
    result = outs[-1]
    for s in range(sections - 1):
        if s in relays:
            hop, via, direct = there[s]
            hop, direct = lax.optimization_barrier((hop, direct))
            there[s] = jnp.concatenate([send(hop, via, s), direct], axis=0)
        result = jnp.where(section == s, there[s], result)
    return result


def solution(mesh):
    in_specs = (
        P(None, "section", "col"),
        P("section", "col", None, None, None),
        P("section", "col", None),
        P("section", "col"),
        P(),
    )
    out_specs = P(None, "section", "col")
    return jax.shard_map(body, mesh=mesh, in_specs=in_specs, out_specs=out_specs, check_vma=False)
```

```python
import functools

import jax
import jax.numpy as jnp
from jax import lax
from jax.experimental import pallas as pl
from jax.experimental.pallas import tpu as pltpu
from jax.sharding import PartitionSpec as P

CAP = 2
CORES = 2
BOTH = ("section", "col")
VM = pl.BlockSpec(memory_space=pltpu.VMEM)
SM = pl.BlockSpec(memory_space=pltpu.SMEM)
HB = pl.BlockSpec(memory_space=pl.ANY)
BIG = 1 << 30


def pool_kernel(cols, blocks_own, src_ref, ask_ref, slot_ref):
    src = src_ref[...]
    owner = src // blocks_own
    slot = jnp.zeros_like(src)
    lows, highs = [], []
    for e in range(cols):
        mine = owner == e
        low = jnp.min(jnp.where(mine, src, BIG), axis=(0, 1), keepdims=True)
        high = jnp.max(jnp.where(mine, src, -1), axis=(0, 1), keepdims=True)
        slot = jnp.where(mine, CAP * e + (src > low).astype(jnp.int32), slot)
        lows.append(low - e * blocks_own)
        highs.append(high - e * blocks_own)
    slot_ref[...] = slot
    for e in range(cols):
        o = e ^ 1
        both = jnp.concatenate([lows[e], highs[e], lows[o], highs[o]], axis=1)
        for s in range(ask_ref.shape[0] // cols):
            ask_ref[s * cols + e] = both


def prepare_kernel(sections, cols, got_ref, slot_ref, sib_slot_ref, w_ref, b_ref, sb_ref, wo_ref, bo_ref, info_ref, sem):
    nxt = jnp.minimum(lax.axis_index("section") + 1, sections - 1)
    need = cols * CAP
    copies = []
    for i in range(need):
        c = got_ref[nxt * cols + i // CAP, 0, i % CAP]
        copies.append(pltpu.make_async_copy(w_ref.at[c], wo_ref.at[i], sem.at[i]))
        copies[-1].start()
    for r, (slots, src) in enumerate(((slot_ref, b_ref), (sib_slot_ref, sb_ref))):
        for i in range(need):
            c = got_ref[nxt * cols + i // CAP, 0, r * CAP + i % CAP]
            bo_ref[r * need + i] = src[c]
            for k in range(slots.shape[0]):
                info_ref[k, r * need + i] = slots[k, c]
            info_ref[slots.shape[0], r * need + i] = c
    for copy in copies:
        copy.wait()


def resident_kernel(sections, w_ref, wv_ref, sem):
    @pl.when(lax.axis_index("section") == sections - 1)
    def _():
        copy = pltpu.make_async_copy(w_ref, wv_ref, sem)
        copy.start()
        copy.wait()


def feature_kernel(cols, got_ref, feat_ref, out_ref):
    batches, rows, _ = feat_ref.shape
    blk = out_ref.shape[3]
    half = batches // CORES
    for z in range(cols // CORES):
        for cd in range(CORES):
            for j in range(CAP):
                b = got_ref[z * CORES + cd, 0, j]
                x = feat_ref[:, :, pl.ds(pl.multiple_of(b * blk, blk), blk)].astype(jnp.float32)
                x = x.reshape(batches * rows, blk).astype(jnp.bfloat16)
                for cp in range(CORES):
                    out_ref[z * CORES + cp, cd * CAP + j] = x[cp * half * rows : (cp + 1) * half * rows]


def way(step, core, zs):
    return (step + core * (zs // 2)) % zs if isinstance(core, int) else lax.rem(step + core * (zs // 2), zs)


def run_layer(zs, blk, core, rel, pool, w, b, info, outs):
    z = lax.axis_index("col") // CORES
    knz = info.shape[0] - 1
    need = zs * CORES * CAP
    cc = lax.rem(core + rel, CORES)
    for dz in range(zs):
        zd = lax.rem(z + way(dz, core, zs), zs)
        for cd in range(CORES):
            for j in range(CAP):
                i = (zd * CORES + cd) * CAP + j
                at = rel * need + i
                x = jnp.concatenate([pool[cc * need + info[k, at]] for k in range(knz)], axis=1)
                y = jnp.dot(x, w[i], preferred_element_type=jnp.float32) + b[at]
                outs[dz][cd * (CORES * CAP) + cc * CAP + j] = jnp.clip(y, 0.0, 32.0).astype(jnp.bfloat16)


def first_kernel(sections, zs, blk, recv_ref, w, b, info, sw_ref, *rest):
    outs, ws, pool, sem = rest[:zs], rest[zs], rest[zs + 1], rest[zs + 2]
    part = recv_ref.shape[2]
    cols = zs * CORES
    need = cols * CAP
    core = lax.rem(lax.axis_index("col"), CORES)
    here = lax.axis_index("section") == 0
    copies = []
    for i in range(need):
        copies.append(pltpu.make_async_copy(sw_ref.at[info[info.shape[0] - 1, need + i]], ws.at[i], sem.at[i]))
        copies[-1].start()

    @pl.when(here)
    def _():
        for s in range(sections):
            for e in range(cols):
                for cd in range(CORES):
                    for j in range(CAP):
                        pool[cd * need + e * CAP + j, s * part : (s + 1) * part] = recv_ref[s * cols + e, cd * CAP + j]
        run_layer(zs, blk, core, 0, pool, w, b, info, outs)

    for copy in copies:
        copy.wait()

    @pl.when(here)
    def _():
        run_layer(zs, blk, core, 1, pool, ws, b, info, outs)


def take_kernel(x_ref, o_ref):
    o_ref[...] = x_ref[...]


def middle_kernel(zs, blk, layer, *refs):
    ins, (w, b, info, ws), outs, pool = refs[:zs], refs[zs : zs + 4], refs[zs + 4 : -1], refs[-1]
    cols = zs * CORES
    z = lax.axis_index("col") // CORES
    core = lax.rem(lax.axis_index("col"), CORES)
    per = CORES * CAP

    @pl.when(lax.axis_index("section") == layer)
    def _():
        for dz in range(zs):
            ze = lax.rem(z - way(dz, core, zs) + zs, zs)
            for cd in range(CORES):
                for q in range(per):
                    pool[cd * cols * CAP + ze * per + q] = ins[dz][cd * per + q]
        run_layer(zs, blk, core, 0, pool, w, b, info, outs)
        run_layer(zs, blk, core, 1, pool, ws, b, info, outs)


def last_kernel(zs, sections, rows_own, mine, first, *refs):
    @pl.when(lax.axis_index("section") == sections - 1)
    def _():
        last_layer(zs, sections, rows_own, mine, first, *refs)


def last_layer(zs, sections, rows_own, mine, first, *refs):
    if first:
        ins, sib, refs = refs[:zs], refs[zs], refs[zs + 1 :]
        slot, rows_ref, w_ref, b_ref, *outs, pool = refs
    else:
        pool, slot, rows_ref, w_ref, b_ref, *outs = refs
    col = lax.axis_index("col")
    z, core = col // CORES, lax.rem(col, CORES)
    per = CORES * CAP
    blk = pool.shape[3]
    batches = rows_ref.shape[0]
    part = pool.shape[2] // CORES
    if first:
        for dz in range(zs):
            ze = lax.rem(z - way(dz, core, zs) + zs, zs)
            zo = lax.rem(z - way(dz, 1 - core, zs) + zs, zs)
            for q in range(per):
                for s in range(sections):
                    rows = slice(s * part, (s + 1) * part)
                    own, other = ins[dz][core * per + q, rows], sib[dz, q, rows]
                    if part % 16 == 0:
                        pool[s, ze * per + q, pl.ds(pl.multiple_of(core * part, part), part), :] = own
                        pool[s, zo * per + q, pl.ds(pl.multiple_of((1 - core) * part, part), part), :] = other
                    else:
                        for h in range(CORES):
                            at = jnp.where(core == h, ze, zo) * per + q
                            pool[s, at, h * part : (h + 1) * part] = jnp.where(core == h, own, other)

    columns, knz = w_ref.shape[0], slot.shape[0]
    ids = lax.broadcasted_iota(jnp.int32, (rows_own, 1), 0)
    live = {s: [(s * rows_own + ids) < rows_ref[m] for m in range(batches)] for s, _ in mine}
    for c in range(columns):
        x = jnp.concatenate(
            [
                jnp.concatenate([pool[s, slot[k, c]] for k in range(knz)], axis=1)
                for s, _ in mine
            ],
            axis=0,
        )
        y = jnp.dot(x, w_ref[c], preferred_element_type=jnp.float32) + b_ref[:, c * blk : (c + 1) * blk]
        y = jnp.clip(y, 0.0, 32.0)
        out = 0
        for n, (s, cuts) in enumerate(mine):
            for m in range(batches):
                at = n * CORES * part + m * rows_own
                t = jnp.where(live[s][m], y[at : at + rows_own], 0.0)
                o, mm = out + m // (batches // cuts), m % (batches // cuts)
                outs[o][mm, :, c * blk : (c + 1) * blk] = t.astype(jnp.bfloat16)
            out += cuts


def body(features, weights, sources, bias, batch_rows):
    sections = lax.axis_size("section")
    cols = lax.axis_size("col")
    zs = cols // CORES
    w = weights[0]
    blocks_own, knz, blk, _ = w.shape
    batches, rows_own, _ = features.shape
    need = cols * CAP
    half = batches * rows_own * sections // CORES
    part = half // sections
    bf, i32, f32 = jnp.bfloat16, jnp.int32, jnp.float32
    S = jax.ShapeDtypeStruct
    section = lax.axis_index("section")

    def room(mib):
        return pltpu.CompilerParams(vmem_limit_bytes=mib << 20)

    ask, slot = pl.pallas_call(
        functools.partial(pool_kernel, cols, blocks_own),
        out_shape=(S((sections * cols, 1, CORES * CAP), i32), S((knz, blocks_own), i32)),
        in_specs=[VM],
        out_specs=(VM, VM),
        compiler_params=room(46),
        name="pools",
    )(sources[0].T)
    got = lax.all_to_all(ask, BOTH, 0, 0, tiled=True)

    total = sections * cols
    sibling = [(i, i ^ 1) for i in range(total)]
    w3 = w.reshape(blocks_own, knz * blk, blk)
    b3 = bias[0].reshape(blocks_own, 1, blk)
    w_then, _ = lax.optimization_barrier((w3, got))
    sw3 = lax.ppermute(w_then, BOTH, sibling)
    sb3 = lax.ppermute(b3, BOTH, sibling)
    sib_slot = lax.ppermute(slot, BOTH, sibling)

    sends = pl.pallas_call(
        functools.partial(feature_kernel, cols),
        out_shape=S((sections * cols, CORES * CAP, part, blk), bf),
        in_specs=[SM, VM],
        out_specs=VM,
        compiler_params=room(56),
        name="gather_features",
    )(got, features)
    recv = lax.all_to_all(sends, BOTH, 0, 0, tiled=True)

    layer_args = pl.pallas_call(
        functools.partial(prepare_kernel, sections, cols),
        out_shape=(S((need, knz * blk, blk), bf), S((CORES * need, 1, blk), f32), S((knz + 1, CORES * need), i32)),
        in_specs=[SM, SM, SM, HB, VM, VM],
        out_specs=(VM, VM, SM),
        scratch_shapes=[pltpu.SemaphoreType.DMA((need,))],
        compiler_params=room(46),
        name="prepare",
    )(got, slot, sib_slot, w3, b3, sb3)
    layer_specs = [VM, VM, SM]
    piece = S((CORES * CORES * CAP, half, blk), bf)
    scratch = [pltpu.VMEM((CORES * need, half, blk), bf)]
    params = room(24)

    def shift(xs, layer):
        def pairs(dz):
            return [(layer * cols + e, (layer + 1) * cols + (e + CORES * way(dz, e % CORES, zs)) % cols) for e in range(cols)]

        order = sorted(range(zs), key=lambda dz: -min(dz, zs - dz))
        ys = {dz: lax.ppermute(xs[dz], BOTH, pairs(dz)) for dz in order}
        if layer == 0:
            order = [*range(1, zs), 0]
        if layer < sections - 2:
            lead, *later = order
            ys[lead] = pl.pallas_call(
                take_kernel, out_shape=piece, in_specs=[VM], out_specs=VM, compiler_params=params, name="take"
            )(ys[lead])
            for dz, y in zip(order, lax.optimization_barrier(tuple(ys[dz] for dz in order))):
                ys[dz] = y
        return [ys[dz] for dz in range(zs)]

    *xs, ws = pl.pallas_call(
        functools.partial(first_kernel, sections, zs, blk),
        out_shape=(piece,) * zs + (S((need, knz * blk, blk), bf),),
        in_specs=[VM] + layer_specs + [HB],
        out_specs=(VM,) * (zs + 1),
        scratch_shapes=scratch + [pltpu.SemaphoreType.DMA((need,))],
        compiler_params=room(44),
        name="first_layer",
    )(recv, *layer_args, sw3)
    xs = shift(xs, 0)
    for layer in range(1, sections - 1):
        xs = pl.pallas_call(
            functools.partial(middle_kernel, zs, blk, layer),
            out_shape=(piece,) * zs,
            in_specs=[VM] * zs + layer_specs + [VM],
            out_specs=(VM,) * zs,
            scratch_shapes=scratch,
            compiler_params=params,
            name="middle_layer",
        )(*xs, *layer_args, ws)
        ready = xs[0]
        xs = shift(xs, layer)

    w_late, _ = lax.optimization_barrier((w3, ready))
    wv = pl.pallas_call(
        functools.partial(resident_kernel, sections),
        out_shape=S(w3.shape, bf),
        in_specs=[HB],
        out_specs=VM,
        scratch_shapes=[pltpu.SemaphoreType.DMA],
        cost_estimate=pl.CostEstimate(flops=0, bytes_accessed=w3.size * 4, transcendentals=0),
        compiler_params=room(40),
        name="resident_weights",
    )(w_late)
    *xs, wv = lax.optimization_barrier((*xs, wv))

    core = lax.rem(lax.axis_index("col"), CORES)
    per = CORES * CAP
    give = jnp.stack([lax.dynamic_slice_in_dim(x, (1 - core) * per, per, 0) for x in xs])
    sib = lax.ppermute(give, BOTH, sibling)

    relays = {0: 1} if sections == 4 and batches % 2 == 0 else {}
    last = sections - 1
    per_section = half * CORES // sections

    def last_call(mine, first, operands, name):
        shapes = [
            S((batches // cuts, rows_own, blocks_own * blk), bf) for _, cuts in mine for _ in range(cuts)
        ]
        if first:
            shapes.append(S((sections, need, per_section, blk), bf))
        return pl.pallas_call(
            functools.partial(last_kernel, zs, sections, rows_own, mine, first),
            out_shape=tuple(shapes),
            in_specs=[VM] * (len(operands) - 4) + [SM, SM, VM, VM],
            out_specs=(VM,) * len(shapes),
            compiler_params=params,
            name=name,
        )(*operands)

    mine = [(s, 2 if s in relays else 1) for s in range(sections)]
    *outs, pool = last_call(mine[:1], True, (*xs, sib, slot, batch_rows, wv, bias), "last_layer")
    outs += last_call(mine[1:], False, (pool, slot, batch_rows, wv, bias), "last_layer_rest")

    def send(x, a, b):
        return lax.ppermute(x, BOTH, [(a * cols + e, b * cols + e) for e in range(cols)])

    there = {}
    for s in range(sections - 1):
        if s in relays:
            via = relays[s]
            hop = send(outs.pop(0), last, via)
            direct = send(outs.pop(0), last, s)
            there[s] = (hop, via, direct)
        else:
            there[s] = send(outs.pop(0), last, s)
    result = outs[-1]
    for s in range(sections - 1):
        if s in relays:
            hop, via, direct = there[s]
            hop, direct = lax.optimization_barrier((hop, direct))
            there[s] = jnp.concatenate([send(hop, via, s), direct], axis=0)
        result = jnp.where(section == s, there[s], result)
    return result


def solution(mesh):
    in_specs = (
        P(None, "section", "col"),
        P("section", "col", None, None, None),
        P("section", "col", None),
        P("section", "col"),
        P(),
    )
    out_specs = P(None, "section", "col")
    return jax.shard_map(body, mesh=mesh, in_specs=in_specs, out_specs=out_specs, check_vma=False)
```

```python
import functools

import jax
import jax.numpy as jnp
from jax import lax
from jax.experimental import pallas as pl
from jax.experimental.pallas import tpu as pltpu
from jax.sharding import PartitionSpec as P

CAP = 2
CORES = 2
BOTH = ("section", "col")
VM = pl.BlockSpec(memory_space=pltpu.VMEM)
SM = pl.BlockSpec(memory_space=pltpu.SMEM)
HB = pl.BlockSpec(memory_space=pl.ANY)
BIG = 1 << 30


def pool_kernel(cols, blocks_own, src_ref, ask_ref, slot_ref):
    src = src_ref[...]
    owner = src // blocks_own
    slot = jnp.zeros_like(src)
    lows, highs = [], []
    for e in range(cols):
        mine = owner == e
        low = jnp.min(jnp.where(mine, src, BIG), axis=(0, 1), keepdims=True)
        high = jnp.max(jnp.where(mine, src, -1), axis=(0, 1), keepdims=True)
        slot = jnp.where(mine, CAP * e + (src > low).astype(jnp.int32), slot)
        lows.append(low - e * blocks_own)
        highs.append(high - e * blocks_own)
    slot_ref[...] = slot
    for e in range(cols):
        o = e ^ 1
        both = jnp.concatenate([lows[e], highs[e], lows[o], highs[o]], axis=1)
        for s in range(ask_ref.shape[0] // cols):
            ask_ref[s * cols + e] = both


def prepare_kernel(sections, cols, got_ref, slot_ref, sib_slot_ref, w_ref, b_ref, sb_ref, wo_ref, bo_ref, info_ref, sem):
    nxt = jnp.minimum(lax.axis_index("section") + 1, sections - 1)
    need = cols * CAP
    copies = []
    for i in range(need):
        c = got_ref[nxt * cols + i // CAP, 0, i % CAP]
        copies.append(pltpu.make_async_copy(w_ref.at[c], wo_ref.at[i], sem.at[i]))
        copies[-1].start()
    for r, (slots, src) in enumerate(((slot_ref, b_ref), (sib_slot_ref, sb_ref))):
        for i in range(need):
            c = got_ref[nxt * cols + i // CAP, 0, r * CAP + i % CAP]
            bo_ref[r * need + i] = src[c]
            for k in range(slots.shape[0]):
                info_ref[k, r * need + i] = slots[k, c]
            info_ref[slots.shape[0], r * need + i] = c
    for copy in copies:
        copy.wait()


def resident_kernel(sections, w_ref, wv_ref, sem):
    @pl.when(lax.axis_index("section") == sections - 1)
    def _():
        copy = pltpu.make_async_copy(w_ref, wv_ref, sem)
        copy.start()
        copy.wait()


def feature_kernel(cols, got_ref, feat_ref, out_ref):
    batches, rows, _ = feat_ref.shape
    blk = out_ref.shape[3]
    half = batches // CORES
    for z in range(cols // CORES):
        for cd in range(CORES):
            for j in range(CAP):
                b = got_ref[z * CORES + cd, 0, j]
                x = feat_ref[:, :, pl.ds(pl.multiple_of(b * blk, blk), blk)].astype(jnp.float32)
                x = x.reshape(batches * rows, blk).astype(jnp.bfloat16)
                for cp in range(CORES):
                    out_ref[z * CORES + cp, cd * CAP + j] = x[cp * half * rows : (cp + 1) * half * rows]


def way(step, core, zs):
    return (step + core * (zs // 2)) % zs if isinstance(core, int) else lax.rem(step + core * (zs // 2), zs)


def run_layer(zs, blk, core, rel, pool, w, b, info, outs):
    z = lax.axis_index("col") // CORES
    knz = info.shape[0] - 1
    need = zs * CORES * CAP
    cc = lax.rem(core + rel, CORES)
    for dz in range(zs):
        zd = lax.rem(z + way(dz, core, zs), zs)
        for cd in range(CORES):
            for j in range(CAP):
                i = (zd * CORES + cd) * CAP + j
                at = rel * need + i
                x = jnp.concatenate([pool[cc * need + info[k, at]] for k in range(knz)], axis=1)
                y = jnp.dot(x, w[i], preferred_element_type=jnp.float32) + b[at]
                outs[dz][cd * (CORES * CAP) + cc * CAP + j] = jnp.clip(y, 0.0, 32.0).astype(jnp.bfloat16)


def first_kernel(sections, zs, blk, recv_ref, w, b, info, sw_ref, *rest):
    outs, ws, pool, sem = rest[:zs], rest[zs], rest[zs + 1], rest[zs + 2]
    part = recv_ref.shape[2]
    cols = zs * CORES
    need = cols * CAP
    core = lax.rem(lax.axis_index("col"), CORES)
    here = lax.axis_index("section") == 0
    copies = []
    for i in range(need):
        copies.append(pltpu.make_async_copy(sw_ref.at[info[info.shape[0] - 1, need + i]], ws.at[i], sem.at[i]))
        copies[-1].start()

    @pl.when(here)
    def _():
        for s in range(sections):
            for e in range(cols):
                for cd in range(CORES):
                    for j in range(CAP):
                        pool[cd * need + e * CAP + j, s * part : (s + 1) * part] = recv_ref[s * cols + e, cd * CAP + j]
        run_layer(zs, blk, core, 0, pool, w, b, info, outs)

    for copy in copies:
        copy.wait()

    @pl.when(here)
    def _():
        run_layer(zs, blk, core, 1, pool, ws, b, info, outs)


def take_kernel(x_ref, o_ref):
    o_ref[...] = x_ref[...]


def middle_kernel(zs, blk, layer, *refs):
    ins, (w, b, info, ws), outs, pool = refs[:zs], refs[zs : zs + 4], refs[zs + 4 : -1], refs[-1]
    cols = zs * CORES
    z = lax.axis_index("col") // CORES
    core = lax.rem(lax.axis_index("col"), CORES)
    per = CORES * CAP

    @pl.when(lax.axis_index("section") == layer)
    def _():
        for dz in range(zs):
            ze = lax.rem(z - way(dz, core, zs) + zs, zs)
            for cd in range(CORES):
                for q in range(per):
                    pool[cd * cols * CAP + ze * per + q] = ins[dz][cd * per + q]
        run_layer(zs, blk, core, 0, pool, w, b, info, outs)
        run_layer(zs, blk, core, 1, pool, ws, b, info, outs)


def last_kernel(zs, sections, rows_own, mine, first, *refs):
    @pl.when(lax.axis_index("section") == sections - 1)
    def _():
        last_layer(zs, sections, rows_own, mine, first, *refs)


def last_layer(zs, sections, rows_own, mine, first, *refs):
    if first:
        ins, sib, refs = refs[:zs], refs[zs], refs[zs + 1 :]
        slot, rows_ref, w_ref, b_ref, *outs, pool = refs
    else:
        pool, slot, rows_ref, w_ref, b_ref, *outs = refs
    col = lax.axis_index("col")
    z, core = col // CORES, lax.rem(col, CORES)
    per = CORES * CAP
    blk = pool.shape[3]
    batches = rows_ref.shape[0]
    part = pool.shape[2] // CORES
    if first:
        for dz in range(zs):
            ze = lax.rem(z - way(dz, core, zs) + zs, zs)
            zo = lax.rem(z - way(dz, 1 - core, zs) + zs, zs)
            for q in range(per):
                for s in range(sections):
                    rows = slice(s * part, (s + 1) * part)
                    own, other = ins[dz][core * per + q, rows], sib[dz, q, rows]
                    if part % 16 == 0:
                        pool[s, ze * per + q, pl.ds(pl.multiple_of(core * part, part), part), :] = own
                        pool[s, zo * per + q, pl.ds(pl.multiple_of((1 - core) * part, part), part), :] = other
                    else:
                        for h in range(CORES):
                            at = jnp.where(core == h, ze, zo) * per + q
                            pool[s, at, h * part : (h + 1) * part] = jnp.where(core == h, own, other)

    columns, knz = w_ref.shape[0], slot.shape[0]
    ids = lax.broadcasted_iota(jnp.int32, (rows_own, 1), 0)
    live = {s: [(s * rows_own + ids) < rows_ref[m] for m in range(batches)] for s, _ in mine}
    for c in range(columns):
        x = jnp.concatenate(
            [
                jnp.concatenate([pool[s, slot[k, c]] for k in range(knz)], axis=1)
                for s, _ in mine
            ],
            axis=0,
        )
        y = jnp.dot(x, w_ref[c], preferred_element_type=jnp.float32) + b_ref[:, c * blk : (c + 1) * blk]
        y = jnp.clip(y, 0.0, 32.0)
        out = 0
        for n, (s, cuts) in enumerate(mine):
            for m in range(batches):
                at = n * CORES * part + m * rows_own
                t = jnp.where(live[s][m], y[at : at + rows_own], 0.0)
                o, mm = out + m // (batches // cuts), m % (batches // cuts)
                outs[o][mm, :, c * blk : (c + 1) * blk] = t.astype(jnp.bfloat16)
            out += cuts


def body(features, weights, sources, bias, batch_rows):
    sections = lax.axis_size("section")
    cols = lax.axis_size("col")
    zs = cols // CORES
    w = weights[0]
    blocks_own, knz, blk, _ = w.shape
    batches, rows_own, _ = features.shape
    need = cols * CAP
    half = batches * rows_own * sections // CORES
    part = half // sections
    bf, i32, f32 = jnp.bfloat16, jnp.int32, jnp.float32
    S = jax.ShapeDtypeStruct
    section = lax.axis_index("section")

    def room(mib):
        return pltpu.CompilerParams(vmem_limit_bytes=mib << 20)

    ask, slot = pl.pallas_call(
        functools.partial(pool_kernel, cols, blocks_own),
        out_shape=(S((sections * cols, 1, CORES * CAP), i32), S((knz, blocks_own), i32)),
        in_specs=[VM],
        out_specs=(VM, VM),
        compiler_params=room(46),
        name="pools",
    )(sources[0].T)
    got = lax.all_to_all(ask, BOTH, 0, 0, tiled=True)

    total = sections * cols
    sibling = [(i, i ^ 1) for i in range(total)]
    w3 = w.reshape(blocks_own, knz * blk, blk)
    b3 = bias[0].reshape(blocks_own, 1, blk)
    w_then, _ = lax.optimization_barrier((w3, got))
    sw3 = lax.ppermute(w_then, BOTH, sibling)
    sb3 = lax.ppermute(b3, BOTH, sibling)
    sib_slot = lax.ppermute(slot, BOTH, sibling)

    sends = pl.pallas_call(
        functools.partial(feature_kernel, cols),
        out_shape=S((sections * cols, CORES * CAP, part, blk), bf),
        in_specs=[SM, VM],
        out_specs=VM,
        compiler_params=room(56),
        name="gather_features",
    )(got, features)
    recv = lax.all_to_all(sends, BOTH, 0, 0, tiled=True)

    layer_args = pl.pallas_call(
        functools.partial(prepare_kernel, sections, cols),
        out_shape=(S((need, knz * blk, blk), bf), S((CORES * need, 1, blk), f32), S((knz + 1, CORES * need), i32)),
        in_specs=[SM, SM, SM, HB, VM, VM],
        out_specs=(VM, VM, SM),
        scratch_shapes=[pltpu.SemaphoreType.DMA((need,))],
        compiler_params=room(46),
        name="prepare",
    )(got, slot, sib_slot, w3, b3, sb3)
    layer_specs = [VM, VM, SM]
    piece = S((CORES * CORES * CAP, half, blk), bf)
    scratch = [pltpu.VMEM((CORES * need, half, blk), bf)]
    params = room(24)

    def shift(xs, layer):
        def pairs(dz):
            return [(layer * cols + e, (layer + 1) * cols + (e + CORES * way(dz, e % CORES, zs)) % cols) for e in range(cols)]

        order = sorted(range(zs), key=lambda dz: -min(dz, zs - dz))
        ys = {dz: lax.ppermute(xs[dz], BOTH, pairs(dz)) for dz in order}
        if 0 < layer < sections - 2:
            order = [*range(1, zs), 0]
            lead, *later = order
            ys[lead] = pl.pallas_call(
                take_kernel, out_shape=piece, in_specs=[VM], out_specs=VM, compiler_params=params, name="take"
            )(ys[lead])
            for dz, y in zip(order, lax.optimization_barrier(tuple(ys[dz] for dz in order))):
                ys[dz] = y
        return [ys[dz] for dz in range(zs)]

    *xs, ws = pl.pallas_call(
        functools.partial(first_kernel, sections, zs, blk),
        out_shape=(piece,) * zs + (S((need, knz * blk, blk), bf),),
        in_specs=[VM] + layer_specs + [HB],
        out_specs=(VM,) * (zs + 1),
        scratch_shapes=scratch + [pltpu.SemaphoreType.DMA((need,))],
        compiler_params=room(44),
        name="first_layer",
    )(recv, *layer_args, sw3)
    xs = shift(xs, 0)
    for layer in range(1, sections - 1):
        xs = pl.pallas_call(
            functools.partial(middle_kernel, zs, blk, layer),
            out_shape=(piece,) * zs,
            in_specs=[VM] * zs + layer_specs + [VM],
            out_specs=(VM,) * zs,
            scratch_shapes=scratch,
            compiler_params=params,
            name="middle_layer",
        )(*xs, *layer_args, ws)
        ready = xs[0]
        xs = shift(xs, layer)

    w_late, _ = lax.optimization_barrier((w3, ready))
    wv = pl.pallas_call(
        functools.partial(resident_kernel, sections),
        out_shape=S(w3.shape, bf),
        in_specs=[HB],
        out_specs=VM,
        scratch_shapes=[pltpu.SemaphoreType.DMA],
        cost_estimate=pl.CostEstimate(flops=0, bytes_accessed=w3.size * 4, transcendentals=0),
        compiler_params=room(40),
        name="resident_weights",
    )(w_late)
    *xs, wv = lax.optimization_barrier((*xs, wv))

    core = lax.rem(lax.axis_index("col"), CORES)
    per = CORES * CAP
    give = jnp.stack([lax.dynamic_slice_in_dim(x, (1 - core) * per, per, 0) for x in xs])
    sib = lax.ppermute(give, BOTH, sibling)

    relays = {0: 1} if sections == 4 and batches % 2 == 0 else {}
    last = sections - 1
    per_section = half * CORES // sections

    def last_call(mine, first, operands, name):
        shapes = [
            S((batches // cuts, rows_own, blocks_own * blk), bf) for _, cuts in mine for _ in range(cuts)
        ]
        if first:
            shapes.append(S((sections, need, per_section, blk), bf))
        return pl.pallas_call(
            functools.partial(last_kernel, zs, sections, rows_own, mine, first),
            out_shape=tuple(shapes),
            in_specs=[VM] * (len(operands) - 4) + [SM, SM, VM, VM],
            out_specs=(VM,) * len(shapes),
            compiler_params=params,
            name=name,
        )(*operands)

    mine = [(s, 2 if s in relays else 1) for s in range(sections)]
    *outs, pool = last_call(mine[:1], True, (*xs, sib, slot, batch_rows, wv, bias), "last_layer")
    outs += last_call(mine[1:], False, (pool, slot, batch_rows, wv, bias), "last_layer_rest")

    def send(x, a, b):
        return lax.ppermute(x, BOTH, [(a * cols + e, b * cols + e) for e in range(cols)])

    there = {}
    for s in range(sections - 1):
        if s in relays:
            via = relays[s]
            hop = send(outs.pop(0), last, via)
            direct = send(outs.pop(0), last, s)
            there[s] = (hop, via, direct)
        else:
            there[s] = send(outs.pop(0), last, s)
    result = outs[-1]
    for s in range(sections - 1):
        if s in relays:
            hop, via, direct = there[s]
            hop, direct = lax.optimization_barrier((hop, direct))
            there[s] = jnp.concatenate([send(hop, via, s), direct], axis=0)
        result = jnp.where(section == s, there[s], result)
    return result


def solution(mesh):
    in_specs = (
        P(None, "section", "col"),
        P("section", "col", None, None, None),
        P("section", "col", None),
        P("section", "col"),
        P(),
    )
    out_specs = P(None, "section", "col")
    return jax.shard_map(body, mesh=mesh, in_specs=in_specs, out_specs=out_specs, check_vma=False)
```
